256 devices in a mesh: dp: 128 (over z, x, y), pair: 2 (over core).
Axes of the slice: x: 4, y: 4, z: 8, core: 2. Of those that a mesh axis runs over, the one named last changes fastest.
Arguments:
- embeddings: float32 [65536, 1024], P(('dp', 'pair')), may hold values from -140 to 140
- block_ids: int32 [128, 2, 512], replicated, may hold values from 0 to 65536, as said below
- block_counts: int32 [128], replicated, may hold values from 0 to 2, as said below
Outputs:
- max_similarity: float32 [65536], P(('dp', 'pair'))
The draws below stay inside these ranges and needn't reach their ends.
Inputs may be any that keep to these rules, and one draw needn't show every extreme that they name: `block_ids`: every document stands in exactly one live slot of one cluster; slots past a cluster's block_counts and the tail of its last block hold 65536; each device gives exactly 4 documents to clusters 2 i and 2 i + 1 together, and at most 4 to one cluster; some cluster takes 4 documents from every device and fills its 2 blocks. `block_counts`: the number of blocks that a cluster's documents fill.
All inputs are finite; a program needn't handle non-finite values.
Results may differ from the reference program's by a relative error of at most 0.0018.
Values may be sent and summed in bfloat16 or wider, within the bound.
No kernel may reach another device: no remote copies, remote signals or barrier semaphores. Data moves between devices by JAX's collectives and lax.ppermute only.
A program may use at most 64 MiB of HBM per device.

```python
import math
from functools import partial
import jax
import jax.numpy as jnp
import numpy as np
from jax import lax

D = 1024
DOC_DEV = 256
BLK = 512
CAP = 4
BMAX = 2
DOCS = 65536
N_DP = 128


def cluster_layout(key):
    key = jax.random.fold_in(key, 5)
    k_level, k_jitter, k_full, k_perm, k_shuffle, k_lone, k_single = jax.random.split(key, 7)
    half_count = N_DP // 2
    sources = 2 * N_DP
    level = jax.random.randint(k_level, (half_count,), 0, CAP + 1)
    spread = max(1, CAP // 8)
    jitter = jax.random.randint(k_jitter, (sources, half_count), -spread, spread + 1)
    full_pair = jax.random.randint(k_full, (), 0, half_count)
    lone_pair = (full_pair + 1 + jax.random.randint(k_lone, (), 0, half_count - 1)) % half_count
    lone_source = jax.random.randint(k_single, (), 0, sources)
    pair_index = jnp.arange(half_count)[None, :]
    source_index = jnp.arange(sources)[:, None]
    doc_share = jnp.clip(level[None, :] + jitter, 0, CAP)
    lone_share = jnp.where(source_index == lone_source, 1, 0)
    doc_share = jnp.where(pair_index == lone_pair, lone_share, doc_share)
    doc_share = jnp.where(pair_index == full_pair, CAP, doc_share)
    local_order = jax.vmap(lambda one_key: jax.random.permutation(one_key, DOC_DEV))(jax.random.split(k_perm, sources))
    position = jnp.arange(DOC_DEV)
    which_pair = position // CAP
    offset = position % CAP
    label_at = 2 * which_pair[None, :] + (offset[None, :] >= doc_share[:, which_pair]).astype(jnp.int32)
    source_rows = jnp.broadcast_to(jnp.arange(sources)[:, None], (sources, DOC_DEV))
    labels = jnp.zeros((sources, DOC_DEV), jnp.int32).at[source_rows, local_order].set(label_at).reshape(-1)
    shuffle = jax.random.permutation(k_shuffle, DOCS)
    doc_order = jnp.argsort(labels * DOCS + shuffle)
    cluster_size = jnp.bincount(labels, length=N_DP)
    offsets = jnp.cumsum(cluster_size) - cluster_size
    slot_index = jnp.arange(BMAX * BLK)
    take_index = jnp.clip(offsets[:, None] + slot_index[None, :], 0, DOCS - 1)
    cluster_ids = jnp.where(slot_index[None, :] < cluster_size[:, None], doc_order[take_index], DOCS)
    counts = (cluster_size + BLK - 1) // BLK
    return (cluster_ids.reshape(N_DP, BMAX, BLK).astype(jnp.int32), counts.astype(jnp.int32))


def draw_block_ids(key, part):
    cluster_ids, counts = cluster_layout(key)
    return cluster_ids


def draw_block_counts(key, part):
    cluster_ids, counts = cluster_layout(key)
    return counts


def shared_scale(key, low, high):
    return jnp.exp(jax.random.uniform(key, (DOCS, 1), jnp.float32, math.log(low), math.log(high)))


def draw_embeddings(key, part):
    key = jax.random.fold_in(key, 11)
    k_noise, k_scale, k_coef = jax.random.split(key, 3)
    noise_part = jnp.clip(jax.random.normal(k_noise, (DOCS, D), jnp.float32), -4.0, 4.0)
    doc_scale = shared_scale(k_scale, 0.3, 3.0)
    shared_part = jnp.clip(jax.random.normal(k_coef, (DOCS, 32), jnp.float32), -4.0, 4.0) * doc_scale * 5.5
    return jnp.concatenate([noise_part[:, :32] + shared_part, noise_part[:, 32:]], axis=1)


def setup_inputs(seed: int = 0) -> dict:
    arg_keys = jax.random.split(jax.random.key(seed), 4)
    return {
        "embeddings": draw_embeddings(jax.random.fold_in(arg_keys[3], 71), 0),
        "block_ids": draw_block_ids(jax.random.fold_in(arg_keys[3], 71), 0),
        "block_counts": draw_block_counts(jax.random.fold_in(arg_keys[3], 71), 0),
    }


def tile_tables(max_blocks):
    first_list = []
    second_list = []
    for second in range(max_blocks):
        for first in range(second + 1):
            first_list.append(first)
            second_list.append(second)
    return (jnp.asarray(np.array(first_list, dtype=np.int32)), jnp.asarray(np.array(second_list, dtype=np.int32)))

def tile_update(members, live_slots, block_rows, first_block, second_block, best_sim):
    start_first = first_block * block_rows
    start_second = second_block * block_rows
    rows_first = lax.dynamic_slice_in_dim(members, start_first, block_rows, 0)
    rows_second = lax.dynamic_slice_in_dim(members, start_second, block_rows, 0)
    live_first = lax.dynamic_slice_in_dim(live_slots, start_first, block_rows, 0)
    live_second = lax.dynamic_slice_in_dim(live_slots, start_second, block_rows, 0)
    scores = jnp.dot(rows_first, rows_second.T, preferred_element_type=jnp.float32)
    within = jnp.arange(block_rows, dtype=jnp.int32)
    same_cell = (first_block == second_block) & (within[:, None] == within[None, :])
    row_best = lax.optimization_barrier(jnp.max(jnp.where(live_second[None, :] & ~same_cell, scores, -1.0), axis=1))
    col_best = lax.optimization_barrier(jnp.max(jnp.where(live_first[:, None] & ~same_cell, scores, -1.0), axis=0))
    old_first = lax.dynamic_slice_in_dim(best_sim, start_first, block_rows, 0)
    best_sim = lax.dynamic_update_slice_in_dim(best_sim, jnp.maximum(old_first, row_best), start_first, 0)
    old_second = lax.dynamic_slice_in_dim(best_sim, start_second, block_rows, 0)
    return lax.dynamic_update_slice_in_dim(best_sim, jnp.maximum(old_second, col_best), start_second, 0)

def keep_same(best_sim):
    return best_sim

def reference(embeddings, block_ids, block_counts):
    square = lax.optimization_barrier(jnp.sum(embeddings * embeddings, axis=1, keepdims=True))
    normed = (embeddings * lax.rsqrt(square + 1e-06)).astype(jnp.bfloat16)
    cluster_total, max_blocks, block_rows = block_ids.shape
    slot_total = max_blocks * block_rows
    doc_total = embeddings.shape[0]
    id_table = block_ids.reshape(cluster_total, slot_total)
    slot_index = jnp.arange(slot_total, dtype=jnp.int32)
    live_table = (slot_index[None, :] // block_rows < block_counts[:, None]) & (id_table < doc_total)
    first_list, second_list = tile_tables(max_blocks)

    def one_cluster(operands):
        cluster_ids, live_slots, live_blocks = operands
        members = jnp.take(normed, jnp.where(live_slots, cluster_ids, doc_total), axis=0, mode='fill', fill_value=0)

        def tile_step(tile_index, best_sim):
            first_block = first_list[tile_index]
            second_block = second_list[tile_index]
            return lax.cond(second_block < live_blocks, partial(tile_update, members, live_slots, block_rows, first_block, second_block), keep_same, best_sim)
        return lax.fori_loop(0, first_list.shape[0], tile_step, jnp.full((slot_total,), -1.0, jnp.float32))
    best_all = lax.map(one_cluster, (id_table, live_table, block_counts))
    target = jnp.where(live_table, id_table, doc_total).reshape(-1)
    return jnp.full((doc_total,), -1.0, jnp.float32).at[target].max(best_all.reshape(-1), mode='drop')
```

```python
from functools import partial

import jax
import jax.numpy as jnp
from jax import lax
from jax.experimental import pallas as pl
from jax.experimental.pallas import tpu as pltpu
from jax.sharding import PartitionSpec as P

BF16 = jnp.bfloat16
F32 = jnp.float32
I32 = jnp.int32
VMEM_LIMIT = 48 * 1024 * 1024


def iota(shape, dim):
    return lax.broadcasted_iota(I32, shape, dim)


def pack_kernel(first_ref, emb_ref, ids_ref, counts_ref, packed_ref, doc_ref):
    doc_rows = emb_ref.shape[0]
    clusters, blocks, block_rows = ids_ref.shape
    doc_total = doc_rows * 2 * clusters
    first = first_ref[0]
    diagonal = iota((clusters, clusters), 0) == iota((clusters, clusters), 1)
    counts = jnp.sum(
        jnp.where(diagonal, jnp.broadcast_to(counts_ref[...], (clusters, clusters)), 0),
        axis=1,
        keepdims=True,
    )
    even = iota((clusters, 1), 0) % 2 == 0
    lift = jnp.where(even, doc_rows, 0)
    keys = []
    for block in range(blocks):
        ids = ids_ref[:, block, :]
        local = ids - first
        mine = (local >= 0) & (local < doc_rows) & (block < counts) & (ids < doc_total)
        keys.append(jnp.where(mine, local + lift, -1).astype(F32))
    lane = iota((clusters, 128), 1)
    even_wide = iota((clusters, 128), 0) % 2 == 0
    picked = jnp.zeros((clusters, 128), F32)
    for rank in range(4):
        best = jnp.maximum(
            jnp.max(keys[0], axis=1, keepdims=True), jnp.max(keys[1], axis=1, keepdims=True)
        )
        wide = jnp.broadcast_to(best, (clusters, 128))
        other = jnp.where(
            even_wide, pltpu.roll(wide, clusters - 1, 0), pltpu.roll(wide, 1, 0)
        )
        top_wide = jnp.maximum(wide, other)
        top = top_wide[:, :1]
        if rank < 3:
            keys = [jnp.where(key == top, -1.0, key) for key in keys]
        doc = jnp.where(top_wide >= doc_rows, top_wide - doc_rows, top_wide)
        picked = jnp.where(lane == rank, doc, picked)
    picked = picked.astype(BF16)
    pairs = clusters // 2
    take_pair = (iota((pairs, clusters), 1) == 2 * iota((pairs, clusters), 0)).astype(BF16)
    doc_ref[...] = jnp.dot(take_pair, picked, preferred_element_type=F32).astype(I32)
    rows = 4 * pairs
    row = iota((rows, clusters), 0)
    spread = (iota((rows, clusters), 1) == 2 * (row // 4)).astype(BF16)
    by_row = jnp.dot(spread, picked, preferred_element_type=F32)
    lane_row = iota((rows, 128), 1) == iota((rows, 128), 0) % 4
    doc_of_row = jnp.sum(jnp.where(lane_row, by_row, 0.0), axis=1, keepdims=True).astype(I32)
    pick = (doc_of_row == iota((rows, doc_rows), 1)).astype(BF16)
    emb = emb_ref[...]
    square = jnp.sum(emb * emb, axis=1, keepdims=True)
    normed = (emb * lax.rsqrt(square + 1e-06)).astype(BF16)
    packed_ref[...] = jnp.dot(pick, normed, preferred_element_type=F32).astype(BF16)


def pack(first, embeddings, block_ids, counts):
    doc_rows, feature = embeddings.shape
    clusters = block_ids.shape[0]
    return pl.pallas_call(
        pack_kernel,
        out_shape=(
            jax.ShapeDtypeStruct((2 * clusters, feature), BF16),
            jax.ShapeDtypeStruct((clusters // 2, 128), I32),
        ),
        in_specs=[
            pl.BlockSpec(memory_space=pltpu.SMEM),
            pl.BlockSpec(memory_space=pltpu.VMEM),
            pl.BlockSpec(memory_space=pltpu.VMEM),
            pl.BlockSpec(memory_space=pltpu.VMEM),
        ],
        out_specs=(
            pl.BlockSpec(memory_space=pltpu.VMEM),
            pl.BlockSpec(memory_space=pltpu.VMEM),
        ),
        compiler_params=pltpu.CompilerParams(vmem_limit_bytes=VMEM_LIMIT),
        name="pack",
    )(first, embeddings, block_ids, counts)


def source_of(chip_base, core, group):
    own = group // 128 == 0
    of_core = jnp.where(own, core, 1 - core)
    hop = jnp.where(of_core == 0, 4, 1)
    chip = jnp.where((group // 64) % 2 == 0, chip_base, chip_base ^ hop)
    return chip * 2 + of_core


def owner_chip(position):
    z, x, half = position // 8, (position // 2) % 4, position % 2
    return z * 16 + x * 4 + half * 2 + (z + x) % 2


def label_kernel(where_ref, ids_ref, counts_ref, row_ref, col_ref):
    _, blocks, block_rows = ids_ref.shape
    core, cluster, doc_rows = where_ref[0], where_ref[1], where_ref[2]
    count = counts_ref[cluster]
    group = iota((256, 1), 0)
    source = source_of(owner_chip(group % 64), core, group)
    hits = jnp.zeros((256, block_rows), F32)
    for block in range(blocks):
        ids = ids_ref[0, block : block + 1, :]
        slot_source = jnp.where(block < count, ids >> 8, -1)
        hits = hits + jnp.where(source == slot_source, 1.0, 0.0)
    tally = jnp.sum(hits, axis=1, keepdims=True)
    tally_wide = jnp.broadcast_to(tally, (256, 128)).astype(BF16)
    col_spread = (iota((1024, 256), 0) // 4 == iota((1024, 256), 1)).astype(BF16)
    by_row = jnp.dot(col_spread, tally_wide, preferred_element_type=F32)
    rank = (iota((1024, 128), 0) % 4).astype(F32)
    col = jnp.where(rank >= by_row, 1.0, 0.0)
    col_ref[...] = col
    row_ref[...] = jnp.transpose(col[:512])[:8]


def labels(where, block_ids, counts):
    clusters, blocks, block_rows = block_ids.shape
    return pl.pallas_call(
        label_kernel,
        out_shape=(
            jax.ShapeDtypeStruct((8, 512), F32),
            jax.ShapeDtypeStruct((1024, 128), F32),
        ),
        grid_spec=pltpu.PrefetchScalarGridSpec(
            num_scalar_prefetch=1,
            grid=(1,),
            in_specs=[
                pl.BlockSpec((1, blocks, block_rows), lambda i, where: (where[1], 0, 0)),
                pl.BlockSpec(memory_space=pltpu.SMEM),
            ],
            out_specs=(
                pl.BlockSpec((8, 512), lambda i, where: (0, 0)),
                pl.BlockSpec((1024, 128), lambda i, where: (0, 0)),
            ),
        ),
        compiler_params=pltpu.CompilerParams(vmem_limit_bytes=VMEM_LIMIT),
        name="labels",
    )(where, block_ids, counts)


def score_kernel(row_ref, col_ref, a_ref, b_ref, c_ref, d_ref, best_ref):
    own = jnp.concatenate([a_ref[...], b_ref[...]], axis=0)
    label = row_ref[0:1, :]
    top = jnp.full((1, 512), -1.0, F32)
    for part, ref in enumerate((a_ref, b_ref, c_ref, d_ref)):
        scores = lax.dot_general(
            ref[...], own, (((1,), (1,)), ((), ())), preferred_element_type=F32
        )
        same = col_ref[part * 256 : (part + 1) * 256, 0:1] == label
        if part < 2:
            same = same & (iota((256, 512), 0) + part * 256 != iota((256, 512), 1))
        top = jnp.maximum(top, jnp.max(jnp.where(same, scores, -1.0), axis=0, keepdims=True))
    slot, member = iota((128, 512), 0), iota((128, 512), 1)
    spread = jnp.where(member // 4 == slot, jnp.broadcast_to(top, (128, 512)), -1.0)
    for rank in range(4):
        best_ref[:, rank : rank + 1] = jnp.max(
            jnp.where(member % 4 == rank, spread, -1.0), axis=1, keepdims=True
        )


def score(row, col, a, b, c, d):
    return pl.pallas_call(
        score_kernel,
        out_shape=jax.ShapeDtypeStruct((128, 4), F32),
        in_specs=[pl.BlockSpec(memory_space=pltpu.VMEM)] * 6,
        out_specs=pl.BlockSpec(memory_space=pltpu.VMEM),
        compiler_params=pltpu.CompilerParams(vmem_limit_bytes=VMEM_LIMIT),
        name="score",
    )(row, col, a, b, c, d)


def unpack_kernel(doc_ref, back_ref, out_ref):
    pairs = doc_ref.shape[0]
    doc_rows = out_ref.shape[1]
    doc_lane = iota((pairs, doc_rows), 1)
    top = jnp.full((pairs, doc_rows), -1.0, F32)
    for rank in range(4):
        hit = doc_ref[:, rank : rank + 1] == doc_lane
        top = jnp.maximum(top, jnp.where(hit, back_ref[0:pairs, rank : rank + 1], -1.0))
    out_ref[...] = jnp.max(top, axis=0, keepdims=True)


def unpack(docs, back, doc_rows):
    return pl.pallas_call(
        unpack_kernel,
        out_shape=jax.ShapeDtypeStruct((1, doc_rows), F32),
        in_specs=[pl.BlockSpec(memory_space=pltpu.VMEM)] * 2,
        out_specs=pl.BlockSpec(memory_space=pltpu.VMEM),
        name="unpack",
    )(docs, back)


def chip_groups():
    owners = [z * 16 + x * 4 + y for z in range(8) for x in range(4) for y in range(4) if (z + x + y) % 2 == 0]
    direct, passing, back, forward, swap = [], [], [], [], []
    for core in range(2):
        hop = 4 if core == 0 else 1
        direct.append([chip * 2 + core for chip in owners])
        passing.append([(chip ^ hop) * 2 + core for chip in owners])
        back.append(direct[-1] + passing[-1])
        forward += list(zip(passing[-1], direct[-1]))
    for chip in range(128):
        swap += [(chip * 2, chip * 2 + 1), (chip * 2 + 1, chip * 2)]
    return direct + passing, back, forward, swap


def body(embeddings, block_ids, block_counts):
    doc_rows, feature = embeddings.shape
    my_chip = lax.axis_index("dp").astype(I32)
    my_core = lax.axis_index("pair").astype(I32)
    send_groups, back_groups, forward, swap = chip_groups()
    both = ("dp", "pair")
    z, x, y = my_chip // 16, (my_chip // 4) % 4, my_chip % 4
    position = z * 8 + x * 2 + y // 2
    first = ((my_chip * 2 + my_core) * doc_rows).reshape(1)
    packed, docs = pack(first, embeddings, block_ids, block_counts.reshape(1, -1))
    packed = packed.reshape(64, 4, feature)
    direct = lax.all_to_all(
        packed, both, split_axis=0, concat_axis=0, axis_index_groups=send_groups, tiled=True
    )
    direct = direct.reshape(256, feature)
    passed = lax.ppermute(direct, both, forward)
    direct_other = lax.ppermute(direct, both, swap)
    where = jnp.stack([my_core, 2 * position, jnp.full_like(my_core, doc_rows)])
    row, col = labels(where, block_ids, block_counts)
    passed_other = lax.ppermute(passed, both, swap)
    best = score(row, col, direct, passed, direct_other, passed_other)
    back = lax.all_to_all(
        best, both, split_axis=0, concat_axis=0, axis_index_groups=back_groups, tiled=True
    )
    return unpack(docs, back, doc_rows).reshape(doc_rows)


def solution(mesh):
    in_specs = (P(("dp", "pair"), None), P(), P())
    out_specs = P(("dp", "pair"))
    return jax.shard_map(body, mesh=mesh, in_specs=in_specs, out_specs=out_specs, check_vma=False)
```

```python
from functools import partial

import jax
import jax.numpy as jnp
from jax import lax
from jax.experimental import pallas as pl
from jax.experimental.pallas import tpu as pltpu
from jax.sharding import PartitionSpec as P

BF16 = jnp.bfloat16
F32 = jnp.float32
I32 = jnp.int32
MIB = 1024 * 1024
BOTH = ("dp", "pair")


def iota(shape, dim):
    return lax.broadcasted_iota(I32, shape, dim)


def in_vmem(count):
    return [pl.BlockSpec(memory_space=pltpu.VMEM)] * count


def my_place():
    return lax.axis_index("dp").astype(I32), lax.axis_index("pair").astype(I32)


def chip_parity(chip):
    return ((chip >> 4) + (chip >> 2) + chip) & 1


def chip_position(chip):
    return chip >> 1


def owner_chip(position):
    return 2 * position + (((position >> 3) + (position >> 1)) & 1)


def pack_kernel(
    emb_hbm, ids_hbm, counts_hbm, packed_ref, doc_ref, emb_ref, ids_ref, counts_ref, sems
):
    copies = [
        pltpu.make_async_copy(counts_hbm, counts_ref, sems.at[0]),
        pltpu.make_async_copy(ids_hbm, ids_ref, sems.at[1]),
        pltpu.make_async_copy(emb_hbm, emb_ref, sems.at[2]),
    ]
    for copy in copies:
        copy.start()
    doc_rows = emb_ref.shape[0]
    clusters, blocks, block_rows = ids_ref.shape
    doc_total = doc_rows * 2 * clusters
    chip, core = my_place()
    first = (chip * 2 + core) * doc_rows
    turned = (chip_parity(chip) == 1) & (chip >= clusters // 2)
    flip = jnp.where(turned, jnp.where(core == 0, 4, 1), 0)
    diagonal = iota((clusters, clusters), 0) == iota((clusters, clusters), 1)
    even = iota((clusters, 1), 0) % 2 == 0
    lift = jnp.where(even, doc_rows, 0)
    lane = iota((clusters, 128), 1)
    even_wide = iota((clusters, 128), 0) % 2 == 0
    copies[0].wait()
    counts = jnp.sum(
        jnp.where(diagonal, jnp.broadcast_to(counts_ref[...], (clusters, clusters)), 0),
        axis=1,
        keepdims=True,
    )
    copies[1].wait()
    keys = []
    for block in range(blocks):
        ids = ids_ref[:, block, :]
        local = ids - first
        mine = (local >= 0) & (local < doc_rows) & (block < counts) & (ids < doc_total)
        keys.append(jnp.where(mine, local + lift, -1).astype(F32))
    picked = jnp.zeros((clusters, 128), F32)
    for rank in range(4):
        best = jnp.max(jnp.maximum(keys[0], keys[1]), axis=1, keepdims=True)
        wide = jnp.broadcast_to(best, (clusters, 128))
        other = jnp.where(
            even_wide, pltpu.roll(wide, clusters - 1, 0), pltpu.roll(wide, 1, 0)
        )
        top_wide = jnp.maximum(wide, other)
        top = top_wide[:, :1]
        if rank < 3:
            keys = [jnp.where(key == top, -1.0, key) for key in keys]
        doc = jnp.where(top_wide >= doc_rows, top_wide - doc_rows, top_wide)
        picked = jnp.where(lane == rank, doc, picked)
    picked = picked.astype(BF16)
    pairs = clusters // 2
    take_pair = (iota((pairs, clusters), 1) == 2 * iota((pairs, clusters), 0)).astype(BF16)
    doc_ref[...] = jnp.dot(take_pair, picked, preferred_element_type=F32).astype(I32)
    rows = 4 * pairs
    row = iota((rows, clusters), 0)
    spread = (iota((rows, clusters), 1) == 2 * ((row >> 2) ^ flip)).astype(BF16)
    by_row = jnp.dot(spread, picked, preferred_element_type=F32)
    lane_row = iota((rows, 128), 1) == iota((rows, 128), 0) % 4
    doc_of_row = jnp.sum(jnp.where(lane_row, by_row, 0.0), axis=1, keepdims=True).astype(I32)
    pick = (doc_of_row == iota((rows, doc_rows), 1)).astype(BF16)
    copies[2].wait()
    emb = emb_ref[...]
    square = jnp.sum(emb * emb, axis=1, keepdims=True)
    normed = (emb * lax.rsqrt(square + 1e-06)).astype(BF16)
    packed_ref[...] = jnp.dot(pick, normed, preferred_element_type=F32).astype(BF16)


def pack(embeddings, block_ids, counts):
    doc_rows, feature = embeddings.shape
    clusters = block_ids.shape[0]
    return pl.pallas_call(
        pack_kernel,
        out_shape=(
            jax.ShapeDtypeStruct((2 * clusters, feature), BF16),
            jax.ShapeDtypeStruct((clusters // 2, 128), I32),
        ),
        in_specs=[pl.BlockSpec(memory_space=pltpu.HBM)] * 3,
        out_specs=tuple(in_vmem(2)),
        scratch_shapes=[
            pltpu.VMEM(embeddings.shape, F32),
            pltpu.VMEM(block_ids.shape, I32),
            pltpu.VMEM(counts.shape, I32),
            pltpu.SemaphoreType.DMA((3,)),
        ],
        compiler_params=pltpu.CompilerParams(vmem_limit_bytes=24 * MIB),
        name="pack",
    )(embeddings, block_ids, counts)


def label_kernel(ids_hbm, counts_hbm, row_ref, col_ref, ids_ref, counts_ref, sems):
    blocks, block_rows = ids_ref.shape
    chip, core = my_place()
    cluster = 2 * chip_position(chip)
    ids_copy = pltpu.make_async_copy(ids_hbm.at[cluster], ids_ref, sems.at[0])
    counts_copy = pltpu.make_async_copy(counts_hbm, counts_ref, sems.at[1])
    ids_copy.start()
    counts_copy.start()
    group = iota((256, 1), 0)
    of_core = jnp.where(group < 128, core, 1 - core)
    hop = jnp.where(of_core == 0, 4, 1)
    base = owner_chip(group & 63)
    source = jnp.where((group & 64) == 0, base, base ^ hop) * 2 + of_core
    counts_copy.wait()
    counts = counts_ref[...]
    count = jnp.sum(jnp.where(iota(counts.shape, 1) == cluster, counts, 0), axis=1, keepdims=True)
    ids_copy.wait()
    hits = jnp.zeros((256, block_rows), F32)
    for block in range(blocks):
        ids = ids_ref[block : block + 1, :]
        slot_source = jnp.where(block < count, ids >> 8, -1)
        hits = hits + jnp.where(source == slot_source, 1.0, 0.0)
    tally = jnp.sum(hits, axis=1, keepdims=True)
    tally_wide = jnp.broadcast_to(tally, (256, 128)).astype(BF16)
    col_spread = (iota((1024, 256), 0) // 4 == iota((1024, 256), 1)).astype(BF16)
    by_row = jnp.dot(col_spread, tally_wide, preferred_element_type=F32)
    rank = (iota((1024, 128), 0) % 4).astype(F32)
    col = jnp.where(rank >= by_row, 1.0, 0.0)
    col_ref[...] = col
    row_ref[...] = jnp.transpose(col[:512])[:8]


def labels(block_ids, counts):
    return pl.pallas_call(
        label_kernel,
        out_shape=(
            jax.ShapeDtypeStruct((8, 512), F32),
            jax.ShapeDtypeStruct((1024, 128), F32),
        ),
        in_specs=[pl.BlockSpec(memory_space=pltpu.HBM)] * 2,
        out_specs=tuple(in_vmem(2)),
        scratch_shapes=[
            pltpu.VMEM(block_ids.shape[1:], I32),
            pltpu.VMEM(counts.shape, I32),
            pltpu.SemaphoreType.DMA((2,)),
        ],
        compiler_params=pltpu.CompilerParams(vmem_limit_bytes=16 * MIB),
        cost_estimate=pl.CostEstimate(flops=10**9, bytes_accessed=4 * MIB, transcendentals=0),
        name="labels",
    )(block_ids, counts)


def column_best(others, own, other_label, own_label, offset=None):
    scores = lax.dot_general(others, own, (((1,), (1,)), ((), ())), preferred_element_type=F32)
    same = other_label == own_label
    if offset is not None:
        same = same & (iota(scores.shape, 0) + offset != iota(scores.shape, 1))
    return jnp.max(jnp.where(same, scores, -1.0), axis=0, keepdims=True)


def direct_kernel(row_ref, col_ref, direct_ref, direct_other_ref, best_ref):
    own = direct_ref[...]
    label = row_ref[0:1, 0:256]
    best = jnp.maximum(
        column_best(own, own, col_ref[0:256, 0:1], label, 0),
        column_best(direct_other_ref[...], own, col_ref[512:768, 0:1], label),
    )
    best_ref[...] = jnp.broadcast_to(best, best_ref.shape)


def passed_kernel(
    row_ref, col_ref, direct_ref, direct_other_ref, low_ref, high_ref, best_direct_ref, best_ref
):
    passed = jnp.concatenate([low_ref[...], high_ref[...]], axis=0)
    own = jnp.concatenate([direct_ref[...], passed], axis=0)
    best = column_best(passed, own, col_ref[256:512, 0:1], row_ref[0:1, :], 256)
    label = row_ref[0:1, 256:512]
    best_passed = jnp.maximum(
        column_best(direct_ref[...], passed, col_ref[0:256, 0:1], label),
        column_best(direct_other_ref[...], passed, col_ref[512:768, 0:1], label),
    )
    best = jnp.maximum(
        best, jnp.concatenate([best_direct_ref[0:1, :], best_passed], axis=1)
    )
    best_ref[...] = jnp.broadcast_to(best, best_ref.shape)


def final_kernel(
    row_ref, col_ref, direct_ref, low_ref, high_ref, low_other_ref, high_other_ref, best_ref, back_ref
):
    own = jnp.concatenate([direct_ref[...], low_ref[...], high_ref[...]], axis=0)
    others = jnp.concatenate([low_other_ref[...], high_other_ref[...]], axis=0)
    best = column_best(others, own, col_ref[768:1024, 0:1], row_ref[0:1, :])
    best = jnp.maximum(best, best_ref[0:1, :])
    slot, member = iota((128, 512), 0), iota((128, 512), 1)
    spread = jnp.where(member // 4 == slot, jnp.broadcast_to(best, (128, 512)), -1.0)
    for rank in range(4):
        back_ref[:, rank : rank + 1] = jnp.max(
            jnp.where(member % 4 == rank, spread, -1.0), axis=1, keepdims=True
        )


def vmem_call(kernel, shape, name, flops, *operands):
    return pl.pallas_call(
        kernel,
        out_shape=jax.ShapeDtypeStruct(shape, F32),
        in_specs=in_vmem(len(operands)),
        out_specs=in_vmem(1)[0],
        compiler_params=pltpu.CompilerParams(vmem_limit_bytes=16 * MIB),
        cost_estimate=pl.CostEstimate(flops=flops, bytes_accessed=2 * MIB, transcendentals=0),
        name=name,
    )(*operands)


def unpack_kernel(doc_ref, back_ref, out_ref):
    pairs = doc_ref.shape[0]
    doc_rows = out_ref.shape[1]
    doc_lane = iota((pairs, doc_rows), 1)
    top = jnp.full((pairs, doc_rows), -1.0, F32)
    for rank in range(4):
        hit = doc_ref[:, rank : rank + 1] == doc_lane
        top = jnp.maximum(top, jnp.where(hit, back_ref[0:pairs, rank : rank + 1], -1.0))
    out_ref[...] = jnp.max(top, axis=0, keepdims=True)


def chip_routes():
    owners = [owner_chip(position) for position in range(64)]
    direct, passing, back = [], [], []
    low, high = [], []
    for core in range(2):
        near, far = (4, 12) if core == 0 else (1, 3)
        direct.append([chip * 2 + core for chip in owners])
        passing.append([(chip ^ near) * 2 + core for chip in owners])
        back.append(direct[-1] + passing[-1])
        low += [((chip ^ near) * 2 + core, chip * 2 + core) for chip in owners]
        high += [((chip ^ far) * 2 + core, chip * 2 + core) for chip in owners]
    swap = []
    for chip in range(128):
        swap += [(chip * 2, chip * 2 + 1), (chip * 2 + 1, chip * 2)]
    return direct + passing, back, low, high, swap


def body(embeddings, block_ids, block_counts):
    doc_rows, feature = embeddings.shape
    send_groups, back_groups, low_route, high_route, swap = chip_routes()
    embeddings = pltpu.with_memory_space_constraint(embeddings, pltpu.HBM)
    block_ids = pltpu.with_memory_space_constraint(block_ids, pltpu.HBM)
    counts = pltpu.with_memory_space_constraint(block_counts.reshape(1, -1), pltpu.HBM)
    packed, docs = pack(embeddings, block_ids, counts)
    packed = packed.reshape(64, 4, feature)
    direct = lax.all_to_all(
        packed, BOTH, split_axis=0, concat_axis=0, axis_index_groups=send_groups, tiled=True
    )
    direct = lax.optimization_barrier(direct.reshape(256, feature))
    low = lax.ppermute(direct[:128], BOTH, low_route)
    high = lax.ppermute(direct[128:], BOTH, high_route)
    direct_other = lax.ppermute(direct, BOTH, swap)
    row, col = labels(block_ids, counts)
    best = vmem_call(
        direct_kernel, (8, 256), "score_direct", 10**9, row, col, direct, direct_other
    )
    low, high, best = lax.optimization_barrier((low, high, best))
    low_other = lax.ppermute(low, BOTH, swap)
    high_other = lax.ppermute(high, BOTH, swap)
    best = vmem_call(
        passed_kernel, (8, 512), "score_passed", 10**9,
        row, col, direct, direct_other, low, high, best,
    )
    best = vmem_call(
        final_kernel, (128, 4), "score_final", 10**9,
        row, col, direct, low, high, low_other, high_other, best,
    )
    back = lax.all_to_all(
        best, BOTH, split_axis=0, concat_axis=0, axis_index_groups=back_groups, tiled=True
    )
    out = pl.pallas_call(
        unpack_kernel,
        out_shape=jax.ShapeDtypeStruct((1, doc_rows), F32),
        in_specs=in_vmem(2),
        out_specs=in_vmem(1)[0],
        compiler_params=pltpu.CompilerParams(vmem_limit_bytes=4 * MIB),
        name="unpack",
    )(docs, back)
    return out.reshape(doc_rows)


def solution(mesh):
    in_specs = (P(("dp", "pair"), None), P(), P())
    out_specs = P(("dp", "pair"))
    return jax.shard_map(body, mesh=mesh, in_specs=in_specs, out_specs=out_specs, check_vma=False)
```

```python
from functools import partial

import jax
import jax.numpy as jnp
from jax import lax
from jax.experimental import pallas as pl
from jax.experimental.pallas import tpu as pltpu
from jax.sharding import PartitionSpec as P

BF16 = jnp.bfloat16
F32 = jnp.float32
I32 = jnp.int32
MIB = 1024 * 1024
BOTH = ("dp", "pair")
LOW = 24


def iota(shape, dim):
    return lax.broadcasted_iota(I32, shape, dim)


def in_vmem(count):
    return [pl.BlockSpec(memory_space=pltpu.VMEM)] * count


def my_place():
    return lax.axis_index("dp").astype(I32), lax.axis_index("pair").astype(I32)


def chip_parity(chip):
    return ((chip >> 4) + (chip >> 2) + chip) & 1


def chip_position(chip):
    return chip >> 1


def owner_chip(position):
    return 2 * position + (((position >> 3) + (position >> 1)) & 1)


def merge_twos(a, b):
    low, high = jnp.minimum(a[0], b[0]), jnp.maximum(a[1], b[1])
    return [
        jnp.maximum(a[0], b[0]), jnp.maximum(low, high), jnp.minimum(low, high), jnp.minimum(a[1], b[1])
    ]


def top_four(a, b):
    c = [jnp.maximum(x, y) for x, y in zip(a, b[::-1])]
    e, f = jnp.maximum(c[0], c[2]), jnp.maximum(c[1], c[3])
    g, h = jnp.minimum(c[0], c[2]), jnp.minimum(c[1], c[3])
    return [jnp.maximum(e, f), jnp.minimum(e, f), jnp.maximum(g, h), jnp.minimum(g, h)]


def pack_kernel(
    emb_hbm, ids_hbm, counts_hbm, packed_ref, doc_ref, emb_ref, ids_ref, counts_ref, sems
):
    copies = [
        pltpu.make_async_copy(counts_hbm, counts_ref, sems.at[0]),
        pltpu.make_async_copy(ids_hbm, ids_ref, sems.at[1]),
        pltpu.make_async_copy(emb_hbm, emb_ref, sems.at[2]),
    ]
    for copy in copies:
        copy.start()
    doc_rows = emb_ref.shape[0]
    clusters = ids_ref.shape[0] // 8
    doc_total = doc_rows * 2 * clusters
    chip, core = my_place()
    first = (chip * 2 + core) * doc_rows
    turned = (chip_parity(chip) == 1) & (chip_position(chip) >= LOW)
    flip = jnp.where(turned, jnp.where(core == 0, 4, 1), 0)
    diagonal = iota((clusters, clusters), 0) == iota((clusters, clusters), 1)
    even = iota((clusters, 1), 0) % 2 == 0
    lift = jnp.where(even, doc_rows, 0)
    even_wide = iota((clusters, 128), 0) % 2 == 0
    copies[0].wait()
    counts = jnp.sum(
        jnp.where(diagonal, jnp.broadcast_to(counts_ref[...], (clusters, clusters)), 0),
        axis=1,
        keepdims=True,
    )
    copies[1].wait()
    tiles = []
    for tile in range(8):
        ids = ids_ref[pl.ds(tile, clusters, stride=8), :]
        local = ids - first
        mine = (local >= 0) & (local < doc_rows) & (tile % 2 < counts) & (ids < doc_total)
        tiles.append(jnp.where(mine, local + lift, -1).astype(F32))
    twos = [(jnp.maximum(a, b), jnp.minimum(a, b)) for a, b in zip(tiles[::2], tiles[1::2])]
    fours = [merge_twos(a, b) for a, b in zip(twos[::2], twos[1::2])]
    mine_top = top_four(*fours)
    partner_top = [
        jnp.where(even_wide, pltpu.roll(a, clusters - 1, 0), pltpu.roll(a, 1, 0)) for a in mine_top
    ]
    ranked = top_four(mine_top, partner_top)
    ranked = [jnp.transpose(a) for a in ranked]
    doc_column = iota((doc_rows, clusters), 0).astype(F32)
    which = iota((clusters, clusters), 0)
    picked = jnp.zeros((clusters, clusters), F32)
    hits = []
    for rank in range(4):
        top = jnp.max(ranked[0], axis=0, keepdims=True)
        hit = ranked[0] == top
        ranked = [jnp.where(hit, b, a) for a, b in zip(ranked, ranked[1:])]
        doc = jnp.where(top >= doc_rows, top - doc_rows, top)
        picked = jnp.where(which == rank, doc, picked)
        hits.append((doc == doc_column).astype(BF16))
    pairs = clusters // 2
    rows = 4 * pairs
    row, spot = iota((rows, 4 * clusters), 0), iota((rows, 4 * clusters), 1)
    spread = (spot == (row & 3) * clusters + 2 * ((row >> 2) ^ flip)).astype(BF16)
    last = (((1,), (1,)), ((), ()))
    pick = lax.dot_general(
        spread, jnp.concatenate(hits, axis=1), last, preferred_element_type=F32
    ).astype(BF16)
    take_pair = (iota((pairs, clusters), 1) == 2 * iota((pairs, clusters), 0)).astype(BF16)
    doc_ref[...] = lax.dot_general(
        take_pair, picked.astype(BF16), last, preferred_element_type=F32
    ).astype(I32)
    copies[2].wait()
    emb = emb_ref[...]
    square = jnp.sum(emb * emb, axis=1, keepdims=True)
    normed = (emb * lax.rsqrt(square + 1e-06)).astype(BF16)
    packed = jnp.dot(pick, normed, preferred_element_type=F32).astype(BF16)
    packed_ref[...] = packed.reshape(packed_ref.shape)


def in_hbm(array):
    return pltpu.with_memory_space_constraint(array, pltpu.HBM)


def pack(embeddings, block_ids, counts):
    clusters, blocks, block_rows = block_ids.shape
    tiles = block_rows // 128
    block_ids = block_ids.reshape(clusters, blocks, tiles, 128).transpose(0, 2, 1, 3)
    block_ids = block_ids.reshape(clusters * tiles * blocks, 128)
    embeddings, block_ids, counts = in_hbm(embeddings), in_hbm(block_ids), in_hbm(counts)
    doc_rows, feature = embeddings.shape
    return pl.pallas_call(
        pack_kernel,
        out_shape=(
            jax.ShapeDtypeStruct((clusters // 2, 4, feature), BF16),
            jax.ShapeDtypeStruct((clusters // 2, 128), I32),
        ),
        in_specs=[pl.BlockSpec(memory_space=pltpu.HBM)] * 3,
        out_specs=tuple(in_vmem(2)),
        scratch_shapes=[
            pltpu.VMEM(embeddings.shape, F32),
            pltpu.VMEM(block_ids.shape, I32),
            pltpu.VMEM(counts.shape, I32),
            pltpu.SemaphoreType.DMA((3,)),
        ],
        compiler_params=pltpu.CompilerParams(vmem_limit_bytes=24 * MIB),
        name="pack",
    )(embeddings, block_ids, counts)


def label_kernel(ids_hbm, counts_hbm, row_ref, col_ref, ids_ref, counts_ref, sems):
    blocks, block_rows = ids_ref.shape
    chip, core = my_place()
    cluster = 2 * chip_position(chip)
    ids_copy = pltpu.make_async_copy(ids_hbm.at[cluster], ids_ref, sems.at[0])
    counts_copy = pltpu.make_async_copy(counts_hbm, counts_ref, sems.at[1])
    ids_copy.start()
    counts_copy.start()
    group = iota((256, 1), 0)
    of_core = jnp.where(group < 128, core, 1 - core)
    hop = jnp.where(of_core == 0, 4, 1)
    base = owner_chip(group & 63)
    source = jnp.where((group & 64) == 0, base, base ^ hop) * 2 + of_core
    counts_copy.wait()
    counts = counts_ref[...]
    count = jnp.sum(jnp.where(iota(counts.shape, 1) == cluster, counts, 0), axis=1, keepdims=True)
    ids_copy.wait()
    hits = jnp.zeros((256, block_rows), F32)
    for block in range(blocks):
        ids = ids_ref[block : block + 1, :]
        slot_source = jnp.where(block < count, ids >> 8, -1)
        hits = hits + jnp.where(source == slot_source, 1.0, 0.0)
    tally = jnp.sum(hits, axis=1, keepdims=True)
    tally_wide = jnp.broadcast_to(tally, (256, 128)).astype(BF16)
    col_spread = (iota((1024, 256), 0) // 4 == iota((1024, 256), 1)).astype(BF16)
    by_row = jnp.dot(col_spread, tally_wide, preferred_element_type=F32)
    rank = (iota((1024, 128), 0) % 4).astype(F32)
    col = jnp.where(rank >= by_row, 1.0, 0.0)
    col_ref[...] = col
    row_ref[...] = jnp.transpose(col[:512])[:8]


def labels(block_ids, counts):
    block_ids, counts = in_hbm(block_ids), in_hbm(counts)
    return pl.pallas_call(
        label_kernel,
        out_shape=(
            jax.ShapeDtypeStruct((8, 512), F32),
            jax.ShapeDtypeStruct((1024, 128), F32),
        ),
        in_specs=[pl.BlockSpec(memory_space=pltpu.HBM)] * 2,
        out_specs=tuple(in_vmem(2)),
        scratch_shapes=[
            pltpu.VMEM(block_ids.shape[1:], I32),
            pltpu.VMEM(counts.shape, I32),
            pltpu.SemaphoreType.DMA((2,)),
        ],
        compiler_params=pltpu.CompilerParams(vmem_limit_bytes=16 * MIB),
        cost_estimate=pl.CostEstimate(flops=10**9, bytes_accessed=4 * MIB, transcendentals=0),
        name="labels",
    )(block_ids, counts)


def column_best(others, own, other_label, own_label, offset=None):
    scores = lax.dot_general(others, own, (((1,), (1,)), ((), ())), preferred_element_type=F32)
    same = other_label == own_label
    if offset is not None:
        same = same & (iota(scores.shape, 0) + offset != iota(scores.shape, 1))
    return jnp.max(jnp.where(same, scores, -1.0), axis=0, keepdims=True)


def rows_of(*refs):
    rows = [ref[...].reshape(4 * ref.shape[0], ref.shape[2]) for ref in refs]
    return rows[0] if len(rows) == 1 else jnp.concatenate(rows, axis=0)


def direct_kernel(row_ref, col_ref, direct_ref, best_ref):
    own = rows_of(direct_ref)
    best = column_best(own, own, col_ref[0:256, 0:1], row_ref[0:1, 0:256], 0)
    best_ref[...] = jnp.broadcast_to(best, best_ref.shape)


def passed_kernel(
    row_ref, col_ref, direct_ref, direct_other_ref, low_ref, high_ref, best_direct_ref, best_ref
):
    direct, passed = rows_of(direct_ref), rows_of(low_ref, high_ref)
    own = jnp.concatenate([direct, passed], axis=0)
    best = jnp.maximum(
        column_best(passed, own, col_ref[256:512, 0:1], row_ref[0:1, :], 256),
        column_best(rows_of(direct_other_ref), own, col_ref[512:768, 0:1], row_ref[0:1, :]),
    )
    best_passed = column_best(direct, passed, col_ref[0:256, 0:1], row_ref[0:1, 256:512])
    best = jnp.maximum(
        best, jnp.concatenate([best_direct_ref[0:1, :], best_passed], axis=1)
    )
    best_ref[...] = jnp.broadcast_to(best, best_ref.shape)


def final_kernel(
    row_ref, col_ref, direct_ref, low_ref, high_ref, low_other_ref, high_other_ref, best_ref, back_ref
):
    own = rows_of(direct_ref, low_ref, high_ref)
    others = rows_of(low_other_ref, high_other_ref)
    best = column_best(others, own, col_ref[768:1024, 0:1], row_ref[0:1, :])
    best = jnp.maximum(best, best_ref[0:1, :])
    slot, member = iota((128, 512), 0), iota((128, 512), 1)
    spread = jnp.where(member // 4 == slot, jnp.broadcast_to(best, (128, 512)), -1.0)
    for rank in range(4):
        back_ref[:, rank : rank + 1] = jnp.max(
            jnp.where(member % 4 == rank, spread, -1.0), axis=1, keepdims=True
        )


def vmem_call(kernel, shape, name, flops, *operands):
    return pl.pallas_call(
        kernel,
        out_shape=jax.ShapeDtypeStruct(shape, F32),
        in_specs=in_vmem(len(operands)),
        out_specs=in_vmem(1)[0],
        compiler_params=pltpu.CompilerParams(vmem_limit_bytes=16 * MIB),
        cost_estimate=pl.CostEstimate(flops=flops, bytes_accessed=2 * MIB, transcendentals=0),
        name=name,
    )(*operands)


def unpack_kernel(doc_ref, back_ref, out_ref):
    pairs = doc_ref.shape[0]
    doc_rows = out_ref.shape[1]
    doc_lane = iota((pairs, doc_rows), 1)
    top = jnp.full((pairs, doc_rows), -1.0, F32)
    for rank in range(4):
        hit = doc_ref[:, rank : rank + 1] == doc_lane
        top = jnp.maximum(top, jnp.where(hit, back_ref[0:pairs, rank : rank + 1], -1.0))
    out_ref[...] = jnp.max(top, axis=0, keepdims=True)


def chip_routes():
    owners = [owner_chip(position) for position in range(64)]
    direct, passing, back = [], [], []
    low, high = [], []
    for core in range(2):
        near, far = (4, 12) if core == 0 else (1, 3)
        direct.append([chip * 2 + core for chip in owners])
        passing.append([(chip ^ near) * 2 + core for chip in owners])
        back.append(direct[-1] + passing[-1])
        low += [((chip ^ near) * 2 + core, chip * 2 + core) for chip in owners]
        high += [((chip ^ far) * 2 + core, chip * 2 + core) for chip in owners]
    swap = [(device, device ^ 1) for device in range(256)]
    owner_swap = [(device, device ^ 1) for device in range(256) if chip_parity(device // 2) == 0]
    return direct + passing, back, low, high, swap, owner_swap


def body(embeddings, block_ids, block_counts):
    doc_rows = embeddings.shape[0]
    send_groups, back_groups, low_route, high_route, swap, owner_swap = chip_routes()
    counts = block_counts.reshape(1, -1)
    packed, docs = pack(embeddings, block_ids, counts)
    direct = lax.all_to_all(
        packed, BOTH, split_axis=0, concat_axis=0, axis_index_groups=send_groups, tiled=True
    )
    high = lax.ppermute(direct[LOW:], BOTH, high_route)
    low = lax.ppermute(direct[:LOW], BOTH, low_route)
    late_ids, late_counts, direct = lax.optimization_barrier((block_ids, counts, direct))
    row, col = labels(late_ids, late_counts)
    direct_other = lax.ppermute(direct, BOTH, swap)
    best = vmem_call(direct_kernel, (8, 256), "score_direct", 10**9, row, col, direct)
    high, best = lax.optimization_barrier((high, best))
    high_other = lax.ppermute(high, BOTH, owner_swap)
    low, best = lax.optimization_barrier((low, best))
    low_other = lax.ppermute(low, BOTH, owner_swap)
    best = vmem_call(
        passed_kernel, (8, 512), "score_passed", 10**9,
        row, col, direct, direct_other, low, high, best,
    )
    best = vmem_call(
        final_kernel, (128, 4), "score_final", 10**9,
        row, col, direct, low, high, low_other, high_other, best,
    )
    back = lax.all_to_all(
        best, BOTH, split_axis=0, concat_axis=0, axis_index_groups=back_groups, tiled=True
    )
    out = pl.pallas_call(
        unpack_kernel,
        out_shape=jax.ShapeDtypeStruct((1, doc_rows), F32),
        in_specs=in_vmem(2),
        out_specs=in_vmem(1)[0],
        compiler_params=pltpu.CompilerParams(vmem_limit_bytes=4 * MIB),
        name="unpack",
    )(docs, back)
    return out.reshape(doc_rows)


def solution(mesh):
    in_specs = (P(("dp", "pair"), None), P(), P())
    out_specs = P(("dp", "pair"))
    return jax.shard_map(body, mesh=mesh, in_specs=in_specs, out_specs=out_specs, check_vma=False)
```

```python
from functools import partial

import jax
import jax.numpy as jnp
from jax import lax
from jax.experimental import pallas as pl
from jax.experimental.pallas import tpu as pltpu
from jax.sharding import PartitionSpec as P

BF16 = jnp.bfloat16
F32 = jnp.float32
I32 = jnp.int32
MIB = 1024 * 1024
BOTH = ("dp", "pair")
LOW = 24


def iota(shape, dim):
    return lax.broadcasted_iota(I32, shape, dim)


def in_vmem(count):
    return [pl.BlockSpec(memory_space=pltpu.VMEM)] * count


def my_place():
    return lax.axis_index("dp").astype(I32), lax.axis_index("pair").astype(I32)


def chip_parity(chip):
    return ((chip >> 4) + (chip >> 2) + chip) & 1


def chip_position(chip):
    return chip >> 1


def owner_chip(position):
    return 2 * position + (((position >> 3) + (position >> 1)) & 1)


def merge_twos(a, b):
    low, high = jnp.minimum(a[0], b[0]), jnp.maximum(a[1], b[1])
    return [
        jnp.maximum(a[0], b[0]), jnp.maximum(low, high), jnp.minimum(low, high), jnp.minimum(a[1], b[1])
    ]


def top_four(a, b):
    c = [jnp.maximum(x, y) for x, y in zip(a, b[::-1])]
    e, f = jnp.maximum(c[0], c[2]), jnp.maximum(c[1], c[3])
    g, h = jnp.minimum(c[0], c[2]), jnp.minimum(c[1], c[3])
    return [jnp.maximum(e, f), jnp.minimum(e, f), jnp.maximum(g, h), jnp.minimum(g, h)]


def pack_kernel(
    emb_hbm, ids_hbm, counts_hbm, packed_ref, doc_ref, emb_ref, ids_ref, counts_ref, sems
):
    copies = [
        pltpu.make_async_copy(counts_hbm, counts_ref, sems.at[0]),
        pltpu.make_async_copy(ids_hbm, ids_ref, sems.at[1]),
        pltpu.make_async_copy(emb_hbm, emb_ref, sems.at[2]),
    ]
    for copy in copies:
        copy.start()
    doc_rows = emb_ref.shape[0]
    clusters = ids_ref.shape[0] // 8
    doc_total = doc_rows * 2 * clusters
    chip, core = my_place()
    first = (chip * 2 + core) * doc_rows
    turned = (chip_parity(chip) == 1) & (chip_position(chip) >= LOW)
    flip = jnp.where(turned, jnp.where(core == 0, 4, 1), 0)
    diagonal = iota((clusters, clusters), 0) == iota((clusters, clusters), 1)
    even = iota((clusters, 1), 0) % 2 == 0
    lift = jnp.where(even, doc_rows, 0)
    even_wide = iota((clusters, 128), 0) % 2 == 0
    copies[0].wait()
    counts = jnp.sum(
        jnp.where(diagonal, jnp.broadcast_to(counts_ref[...], (clusters, clusters)), 0),
        axis=1,
        keepdims=True,
    )
    copies[1].wait()
    tiles = []
    for tile in range(8):
        ids = ids_ref[pl.ds(tile, clusters, stride=8), :]
        local = ids - first
        mine = (local >= 0) & (local < doc_rows) & (tile % 2 < counts) & (ids < doc_total)
        tiles.append(jnp.where(mine, local + lift, -1).astype(F32))
    twos = [(jnp.maximum(a, b), jnp.minimum(a, b)) for a, b in zip(tiles[::2], tiles[1::2])]
    fours = [merge_twos(a, b) for a, b in zip(twos[::2], twos[1::2])]
    mine_top = top_four(*fours)
    partner_top = [
        jnp.where(even_wide, pltpu.roll(a, clusters - 1, 0), pltpu.roll(a, 1, 0)) for a in mine_top
    ]
    ranked = top_four(mine_top, partner_top)
    ranked = [jnp.transpose(a) for a in ranked]
    doc_column = iota((doc_rows, clusters), 0).astype(F32)
    which = iota((clusters, clusters), 0)
    picked = jnp.zeros((clusters, clusters), F32)
    hits = []
    for rank in range(4):
        top = jnp.max(ranked[0], axis=0, keepdims=True)
        hit = ranked[0] == top
        ranked = [jnp.where(hit, b, a) for a, b in zip(ranked, ranked[1:])]
        doc = jnp.where(top >= doc_rows, top - doc_rows, top)
        picked = jnp.where(which == rank, doc, picked)
        hits.append((doc == doc_column).astype(BF16))
    pairs = clusters // 2
    rows = 4 * pairs
    row, spot = iota((rows, 4 * clusters), 0), iota((rows, 4 * clusters), 1)
    spread = (spot == (row & 3) * clusters + 2 * ((row >> 2) ^ flip)).astype(BF16)
    last = (((1,), (1,)), ((), ()))
    pick = lax.dot_general(
        spread, jnp.concatenate(hits, axis=1), last, preferred_element_type=F32
    ).astype(BF16)
    take_pair = (iota((pairs, clusters), 1) == 2 * iota((pairs, clusters), 0)).astype(BF16)
    doc_ref[...] = lax.dot_general(
        take_pair, picked.astype(BF16), last, preferred_element_type=F32
    ).astype(I32)
    copies[2].wait()
    emb = emb_ref[...]
    square = jnp.sum(emb * emb, axis=1, keepdims=True)
    normed = (emb * lax.rsqrt(square + 1e-06)).astype(BF16)
    packed = jnp.dot(pick, normed, preferred_element_type=F32).astype(BF16)
    packed_ref[...] = packed.reshape(packed_ref.shape)


def in_hbm(array):
    return pltpu.with_memory_space_constraint(array, pltpu.HBM)


def pack(embeddings, block_ids, counts):
    clusters, blocks, block_rows = block_ids.shape
    tiles = block_rows // 128
    block_ids = block_ids.reshape(clusters, blocks, tiles, 128).transpose(0, 2, 1, 3)
    block_ids = block_ids.reshape(clusters * tiles * blocks, 128)
    embeddings, block_ids, counts = in_hbm(embeddings), in_hbm(block_ids), in_hbm(counts)
    doc_rows, feature = embeddings.shape
    return pl.pallas_call(
        pack_kernel,
        out_shape=(
            jax.ShapeDtypeStruct((clusters // 2, 4, feature), BF16),
            jax.ShapeDtypeStruct((clusters // 2, 128), I32),
        ),
        in_specs=[pl.BlockSpec(memory_space=pltpu.HBM)] * 3,
        out_specs=tuple(in_vmem(2)),
        scratch_shapes=[
            pltpu.VMEM(embeddings.shape, F32),
            pltpu.VMEM(block_ids.shape, I32),
            pltpu.VMEM(counts.shape, I32),
            pltpu.SemaphoreType.DMA((3,)),
        ],
        compiler_params=pltpu.CompilerParams(vmem_limit_bytes=24 * MIB),
        name="pack",
    )(embeddings, block_ids, counts)


def label_kernel(ids_hbm, counts_hbm, row_ref, col_ref, ids_ref, counts_ref, sems):
    blocks, block_rows = ids_ref.shape
    chip, core = my_place()
    cluster = 2 * chip_position(chip)
    ids_copy = pltpu.make_async_copy(ids_hbm.at[cluster], ids_ref, sems.at[0])
    counts_copy = pltpu.make_async_copy(counts_hbm, counts_ref, sems.at[1])
    ids_copy.start()
    counts_copy.start()
    group = iota((256, 1), 0)
    of_core = jnp.where(group < 128, core, 1 - core)
    hop = jnp.where(of_core == 0, 4, 1)
    base = owner_chip(group & 63)
    source = jnp.where((group & 64) == 0, base, base ^ hop) * 2 + of_core
    counts_copy.wait()
    counts = counts_ref[...]
    count = jnp.sum(jnp.where(iota(counts.shape, 1) == cluster, counts, 0), axis=1, keepdims=True)
    ids_copy.wait()
    hits = jnp.zeros((256, block_rows), F32)
    for block in range(blocks):
        ids = ids_ref[block : block + 1, :]
        slot_source = jnp.where(block < count, ids >> 8, -1)
        hits = hits + jnp.where(source == slot_source, 1.0, 0.0)
    tally = jnp.sum(hits, axis=1, keepdims=True)
    tally_wide = jnp.broadcast_to(tally, (256, 128)).astype(BF16)
    col_spread = (iota((1024, 256), 0) // 4 == iota((1024, 256), 1)).astype(BF16)
    by_row = jnp.dot(col_spread, tally_wide, preferred_element_type=F32)
    rank = (iota((1024, 128), 0) % 4).astype(F32)
    col = jnp.where(rank >= by_row, 1.0, 0.0)
    col_ref[...] = col
    row_ref[...] = jnp.transpose(col[:512])[:8]


def labels(block_ids, counts):
    block_ids, counts = in_hbm(block_ids), in_hbm(counts)
    return pl.pallas_call(
        label_kernel,
        out_shape=(
            jax.ShapeDtypeStruct((8, 512), F32),
            jax.ShapeDtypeStruct((1024, 128), F32),
        ),
        in_specs=[pl.BlockSpec(memory_space=pltpu.HBM)] * 2,
        out_specs=tuple(in_vmem(2)),
        scratch_shapes=[
            pltpu.VMEM(block_ids.shape[1:], I32),
            pltpu.VMEM(counts.shape, I32),
            pltpu.SemaphoreType.DMA((2,)),
        ],
        compiler_params=pltpu.CompilerParams(vmem_limit_bytes=16 * MIB),
        cost_estimate=pl.CostEstimate(flops=10**9, bytes_accessed=4 * MIB, transcendentals=0),
        name="labels",
    )(block_ids, counts)


def column_best(others, own, other_label, own_label, offset=None):
    scores = lax.dot_general(others, own, (((1,), (1,)), ((), ())), preferred_element_type=F32)
    same = other_label == own_label
    if offset is not None:
        same = same & (iota(scores.shape, 0) + offset != iota(scores.shape, 1))
    return jnp.max(jnp.where(same, scores, -1.0), axis=0, keepdims=True)


def rows_of(*refs):
    rows = [ref[...].reshape(4 * ref.shape[0], ref.shape[2]) for ref in refs]
    return rows[0] if len(rows) == 1 else jnp.concatenate(rows, axis=0)


def direct_kernel(row_ref, col_ref, direct_ref, direct_other_ref, best_ref):
    own = rows_of(direct_ref)
    label = row_ref[0:1, 0:256]
    best = jnp.maximum(
        column_best(own, own, col_ref[0:256, 0:1], label, 0),
        column_best(rows_of(direct_other_ref), own, col_ref[512:768, 0:1], label),
    )
    best_ref[...] = jnp.broadcast_to(best, best_ref.shape)


def passed_kernel(
    row_ref, col_ref, direct_ref, direct_other_ref, low_ref, high_ref, best_direct_ref, best_ref
):
    direct, passed = rows_of(direct_ref), rows_of(low_ref, high_ref)
    own = jnp.concatenate([direct, passed], axis=0)
    best = column_best(passed, own, col_ref[256:512, 0:1], row_ref[0:1, :], 256)
    label = row_ref[0:1, 256:512]
    best_passed = jnp.maximum(
        column_best(direct, passed, col_ref[0:256, 0:1], label),
        column_best(rows_of(direct_other_ref), passed, col_ref[512:768, 0:1], label),
    )
    best = jnp.maximum(
        best, jnp.concatenate([best_direct_ref[0:1, :], best_passed], axis=1)
    )
    best_ref[...] = jnp.broadcast_to(best, best_ref.shape)


def final_kernel(
    row_ref, col_ref, direct_ref, low_ref, high_ref, low_other_ref, high_other_ref, best_ref, back_ref
):
    own = rows_of(direct_ref, low_ref, high_ref)
    others = rows_of(low_other_ref, high_other_ref)
    best = column_best(others, own, col_ref[768:1024, 0:1], row_ref[0:1, :])
    best = jnp.maximum(best, best_ref[0:1, :])
    slot, member = iota((128, 512), 0), iota((128, 512), 1)
    spread = jnp.where(member // 4 == slot, jnp.broadcast_to(best, (128, 512)), -1.0)
    for rank in range(4):
        back_ref[:, rank : rank + 1] = jnp.max(
            jnp.where(member % 4 == rank, spread, -1.0), axis=1, keepdims=True
        )


def vmem_call(kernel, shape, name, flops, *operands):
    return pl.pallas_call(
        kernel,
        out_shape=jax.ShapeDtypeStruct(shape, F32),
        in_specs=in_vmem(len(operands)),
        out_specs=in_vmem(1)[0],
        compiler_params=pltpu.CompilerParams(vmem_limit_bytes=16 * MIB),
        cost_estimate=pl.CostEstimate(flops=flops, bytes_accessed=2 * MIB, transcendentals=0),
        name=name,
    )(*operands)


def unpack_kernel(doc_ref, back_ref, out_ref):
    pairs = doc_ref.shape[0]
    doc_rows = out_ref.shape[1]
    doc_lane = iota((pairs, doc_rows), 1)
    top = jnp.full((pairs, doc_rows), -1.0, F32)
    for rank in range(4):
        hit = doc_ref[:, rank : rank + 1] == doc_lane
        top = jnp.maximum(top, jnp.where(hit, back_ref[0:pairs, rank : rank + 1], -1.0))
    out_ref[...] = jnp.max(top, axis=0, keepdims=True)


def chip_routes():
    owners = [owner_chip(position) for position in range(64)]
    direct, passing, back = [], [], []
    low, high = [], []
    for core in range(2):
        near, far = (4, 12) if core == 0 else (1, 3)
        direct.append([chip * 2 + core for chip in owners])
        passing.append([(chip ^ near) * 2 + core for chip in owners])
        back.append(direct[-1] + passing[-1])
        low += [((chip ^ near) * 2 + core, chip * 2 + core) for chip in owners]
        high += [((chip ^ far) * 2 + core, chip * 2 + core) for chip in owners]
    swap = [(device, device ^ 1) for device in range(256)]
    owner_swap = [(device, device ^ 1) for device in range(256) if chip_parity(device // 2) == 0]
    return direct + passing, back, low, high, swap, owner_swap


def body(embeddings, block_ids, block_counts):
    doc_rows = embeddings.shape[0]
    send_groups, back_groups, low_route, high_route, swap, owner_swap = chip_routes()
    counts = block_counts.reshape(1, -1)
    packed, docs = pack(embeddings, block_ids, counts)
    direct = lax.all_to_all(
        packed, BOTH, split_axis=0, concat_axis=0, axis_index_groups=send_groups, tiled=True
    )
    high = lax.ppermute(direct[LOW:], BOTH, high_route)
    low = lax.ppermute(direct[:LOW], BOTH, low_route)
    late_ids, late_counts, direct = lax.optimization_barrier((block_ids, counts, direct))
    row, col = labels(late_ids, late_counts)
    direct_other = lax.ppermute(direct, BOTH, swap)
    best = vmem_call(
        direct_kernel, (8, 256), "score_direct", 10**9, row, col, direct, direct_other
    )
    low, high, best = lax.optimization_barrier((low, high, best))
    low_other = lax.ppermute(low, BOTH, owner_swap)
    high_other = lax.ppermute(high, BOTH, owner_swap)
    best = vmem_call(
        passed_kernel, (8, 512), "score_passed", 10**9,
        row, col, direct, direct_other, low, high, best,
    )
    best = vmem_call(
        final_kernel, (128, 4), "score_final", 10**9,
        row, col, direct, low, high, low_other, high_other, best,
    )
    back = lax.all_to_all(
        best, BOTH, split_axis=0, concat_axis=0, axis_index_groups=back_groups, tiled=True
    )
    out = pl.pallas_call(
        unpack_kernel,
        out_shape=jax.ShapeDtypeStruct((1, doc_rows), F32),
        in_specs=in_vmem(2),
        out_specs=in_vmem(1)[0],
        compiler_params=pltpu.CompilerParams(vmem_limit_bytes=4 * MIB),
        name="unpack",
    )(docs, back)
    return out.reshape(doc_rows)


def solution(mesh):
    in_specs = (P(("dp", "pair"), None), P(), P())
    out_specs = P(("dp", "pair"))
    return jax.shard_map(body, mesh=mesh, in_specs=in_specs, out_specs=out_specs, check_vma=False)
```

```python
from functools import partial

import jax
import jax.numpy as jnp
from jax import lax
from jax.experimental import pallas as pl
from jax.experimental.pallas import tpu as pltpu
from jax.sharding import PartitionSpec as P

BF16 = jnp.bfloat16
F32 = jnp.float32
I32 = jnp.int32
MIB = 1024 * 1024
BOTH = ("dp", "pair")
LOW = 24


def iota(shape, dim):
    return lax.broadcasted_iota(I32, shape, dim)


def in_vmem(count):
    return [pl.BlockSpec(memory_space=pltpu.VMEM)] * count


def my_place():
    return lax.axis_index("dp").astype(I32), lax.axis_index("pair").astype(I32)


def chip_parity(chip):
    return ((chip >> 4) + (chip >> 2) + chip) & 1


def chip_position(chip):
    return chip >> 1


def owner_chip(position):
    return 2 * position + (((position >> 3) + (position >> 1)) & 1)


def merge_twos(a, b):
    low, high = jnp.minimum(a[0], b[0]), jnp.maximum(a[1], b[1])
    return [
        jnp.maximum(a[0], b[0]), jnp.maximum(low, high), jnp.minimum(low, high), jnp.minimum(a[1], b[1])
    ]


def top_four(a, b):
    c = [jnp.maximum(x, y) for x, y in zip(a, b[::-1])]
    e, f = jnp.maximum(c[0], c[2]), jnp.maximum(c[1], c[3])
    g, h = jnp.minimum(c[0], c[2]), jnp.minimum(c[1], c[3])
    return [jnp.maximum(e, f), jnp.minimum(e, f), jnp.maximum(g, h), jnp.minimum(g, h)]


def pack_kernel(
    emb_hbm, ids_hbm, counts_hbm, packed_ref, doc_ref, emb_ref, ids_ref, counts_ref, sems
):
    copies = [
        pltpu.make_async_copy(counts_hbm, counts_ref, sems.at[0]),
        pltpu.make_async_copy(ids_hbm, ids_ref, sems.at[1]),
        pltpu.make_async_copy(emb_hbm, emb_ref, sems.at[2]),
    ]
    for copy in copies:
        copy.start()
    doc_rows = emb_ref.shape[0]
    clusters = ids_ref.shape[0] // 8
    doc_total = doc_rows * 2 * clusters
    chip, core = my_place()
    first = (chip * 2 + core) * doc_rows
    turned = (chip_parity(chip) == 1) & (chip_position(chip) >= LOW)
    flip = jnp.where(turned, jnp.where(core == 0, 4, 1), 0)
    diagonal = iota((clusters, clusters), 0) == iota((clusters, clusters), 1)
    even = iota((clusters, 1), 0) % 2 == 0
    lift = jnp.where(even, doc_rows, 0)
    even_wide = iota((clusters, 128), 0) % 2 == 0
    copies[0].wait()
    counts = jnp.sum(
        jnp.where(diagonal, jnp.broadcast_to(counts_ref[...], (clusters, clusters)), 0),
        axis=1,
        keepdims=True,
    )
    copies[1].wait()
    tiles = []
    for tile in range(8):
        ids = ids_ref[pl.ds(tile, clusters, stride=8), :]
        local = ids - first
        mine = (local >= 0) & (local < doc_rows) & (tile % 2 < counts) & (ids < doc_total)
        tiles.append(jnp.where(mine, local + lift, -1).astype(F32))
    twos = [(jnp.maximum(a, b), jnp.minimum(a, b)) for a, b in zip(tiles[::2], tiles[1::2])]
    fours = [merge_twos(a, b) for a, b in zip(twos[::2], twos[1::2])]
    mine_top = top_four(*fours)
    partner_top = [
        jnp.where(even_wide, pltpu.roll(a, clusters - 1, 0), pltpu.roll(a, 1, 0)) for a in mine_top
    ]
    ranked = top_four(mine_top, partner_top)
    ranked = [jnp.transpose(a) for a in ranked]
    doc_column = iota((doc_rows, clusters), 0).astype(F32)
    which = iota((clusters, clusters), 0)
    picked = jnp.zeros((clusters, clusters), F32)
    hits = []
    for rank in range(4):
        top = jnp.max(ranked[0], axis=0, keepdims=True)
        hit = ranked[0] == top
        ranked = [jnp.where(hit, b, a) for a, b in zip(ranked, ranked[1:])]
        doc = jnp.where(top >= doc_rows, top - doc_rows, top)
        picked = jnp.where(which == rank, doc, picked)
        hits.append((doc == doc_column).astype(BF16))
    pairs = clusters // 2
    rows = 4 * pairs
    row, spot = iota((rows, 4 * clusters), 0), iota((rows, 4 * clusters), 1)
    spread = (spot == (row & 3) * clusters + 2 * ((row >> 2) ^ flip)).astype(BF16)
    last = (((1,), (1,)), ((), ()))
    pick = lax.dot_general(
        spread, jnp.concatenate(hits, axis=1), last, preferred_element_type=F32
    ).astype(BF16)
    take_pair = (iota((pairs, clusters), 1) == 2 * iota((pairs, clusters), 0)).astype(BF16)
    doc_ref[...] = lax.dot_general(
        take_pair, picked.astype(BF16), last, preferred_element_type=F32
    ).astype(I32)
    copies[2].wait()
    emb = emb_ref[...]
    square = jnp.sum(emb * emb, axis=1, keepdims=True)
    normed = (emb * lax.rsqrt(square + 1e-06)).astype(BF16)
    packed = jnp.dot(pick, normed, preferred_element_type=F32).astype(BF16)
    packed_ref[...] = packed.reshape(packed_ref.shape)


def in_hbm(array):
    return pltpu.with_memory_space_constraint(array, pltpu.HBM)


def pack(embeddings, block_ids, counts):
    clusters, blocks, block_rows = block_ids.shape
    tiles = block_rows // 128
    block_ids = block_ids.reshape(clusters, blocks, tiles, 128).transpose(0, 2, 1, 3)
    block_ids = block_ids.reshape(clusters * tiles * blocks, 128)
    embeddings, block_ids, counts = in_hbm(embeddings), in_hbm(block_ids), in_hbm(counts)
    doc_rows, feature = embeddings.shape
    return pl.pallas_call(
        pack_kernel,
        out_shape=(
            jax.ShapeDtypeStruct((clusters // 2, 4, feature), BF16),
            jax.ShapeDtypeStruct((clusters // 2, 128), I32),
        ),
        in_specs=[pl.BlockSpec(memory_space=pltpu.HBM)] * 3,
        out_specs=tuple(in_vmem(2)),
        scratch_shapes=[
            pltpu.VMEM(embeddings.shape, F32),
            pltpu.VMEM(block_ids.shape, I32),
            pltpu.VMEM(counts.shape, I32),
            pltpu.SemaphoreType.DMA((3,)),
        ],
        compiler_params=pltpu.CompilerParams(vmem_limit_bytes=24 * MIB),
        name="pack",
    )(embeddings, block_ids, counts)


def label_kernel(ids_hbm, counts_hbm, row_ref, col_ref, ids_ref, counts_ref, sems):
    blocks, block_rows = ids_ref.shape
    chip, core = my_place()
    cluster = 2 * chip_position(chip)
    ids_copy = pltpu.make_async_copy(ids_hbm.at[cluster], ids_ref, sems.at[0])
    counts_copy = pltpu.make_async_copy(counts_hbm, counts_ref, sems.at[1])
    ids_copy.start()
    counts_copy.start()
    group = iota((256, 1), 0)
    of_core = jnp.where(group < 128, core, 1 - core)
    hop = jnp.where(of_core == 0, 4, 1)
    base = owner_chip(group & 63)
    source = jnp.where((group & 64) == 0, base, base ^ hop) * 2 + of_core
    counts_copy.wait()
    counts = counts_ref[...]
    count = jnp.sum(jnp.where(iota(counts.shape, 1) == cluster, counts, 0), axis=1, keepdims=True)
    ids_copy.wait()
    hits = jnp.zeros((256, block_rows), F32)
    for block in range(blocks):
        ids = ids_ref[block : block + 1, :]
        slot_source = jnp.where(block < count, ids >> 8, -1)
        hits = hits + jnp.where(source == slot_source, 1.0, 0.0)
    tally = jnp.sum(hits, axis=1, keepdims=True)
    tally_wide = jnp.broadcast_to(tally, (256, 128)).astype(BF16)
    col_spread = (iota((1024, 256), 0) // 4 == iota((1024, 256), 1)).astype(BF16)
    by_row = jnp.dot(col_spread, tally_wide, preferred_element_type=F32)
    rank = (iota((1024, 128), 0) % 4).astype(F32)
    col = jnp.where(rank >= by_row, 1.0, 0.0)
    col_ref[...] = col
    row_ref[...] = jnp.transpose(col[:512])[:8]


def labels(block_ids, counts):
    block_ids, counts = in_hbm(block_ids), in_hbm(counts)
    return pl.pallas_call(
        label_kernel,
        out_shape=(
            jax.ShapeDtypeStruct((8, 512), F32),
            jax.ShapeDtypeStruct((1024, 128), F32),
        ),
        in_specs=[pl.BlockSpec(memory_space=pltpu.HBM)] * 2,
        out_specs=tuple(in_vmem(2)),
        scratch_shapes=[
            pltpu.VMEM(block_ids.shape[1:], I32),
            pltpu.VMEM(counts.shape, I32),
            pltpu.SemaphoreType.DMA((2,)),
        ],
        compiler_params=pltpu.CompilerParams(vmem_limit_bytes=16 * MIB),
        cost_estimate=pl.CostEstimate(flops=10**9, bytes_accessed=4 * MIB, transcendentals=0),
        name="labels",
    )(block_ids, counts)


def column_best(others, own, other_label, own_label, offset=None):
    scores = lax.dot_general(others, own, (((1,), (1,)), ((), ())), preferred_element_type=F32)
    same = other_label == own_label
    if offset is not None:
        same = same & (iota(scores.shape, 0) + offset != iota(scores.shape, 1))
    return jnp.max(jnp.where(same, scores, -1.0), axis=0, keepdims=True)


def rows_of(*refs):
    rows = [ref[...].reshape(4 * ref.shape[0], ref.shape[2]) for ref in refs]
    return rows[0] if len(rows) == 1 else jnp.concatenate(rows, axis=0)


def direct_kernel(row_ref, col_ref, direct_ref, direct_other_ref, best_ref):
    own = rows_of(direct_ref)
    label = row_ref[0:1, 0:256]
    best = jnp.maximum(
        column_best(own, own, col_ref[0:256, 0:1], label, 0),
        column_best(rows_of(direct_other_ref), own, col_ref[512:768, 0:1], label),
    )
    best_ref[...] = jnp.broadcast_to(best, best_ref.shape)


def passed_kernel(
    row_ref, col_ref, direct_ref, direct_other_ref, low_ref, high_ref, best_direct_ref, best_ref
):
    direct, passed = rows_of(direct_ref), rows_of(low_ref, high_ref)
    own = jnp.concatenate([direct, passed], axis=0)
    best = column_best(passed, own, col_ref[256:512, 0:1], row_ref[0:1, :], 256)
    label = row_ref[0:1, 256:512]
    best_passed = jnp.maximum(
        column_best(direct, passed, col_ref[0:256, 0:1], label),
        column_best(rows_of(direct_other_ref), passed, col_ref[512:768, 0:1], label),
    )
    best = jnp.maximum(
        best, jnp.concatenate([best_direct_ref[0:1, :], best_passed], axis=1)
    )
    best_ref[...] = jnp.broadcast_to(best, best_ref.shape)


def final_kernel(
    row_ref, col_ref, direct_ref, low_ref, high_ref, low_other_ref, high_other_ref, best_ref, back_ref
):
    own = rows_of(direct_ref, low_ref, high_ref)
    others = rows_of(low_other_ref, high_other_ref)
    best = column_best(others, own, col_ref[768:1024, 0:1], row_ref[0:1, :])
    best = jnp.maximum(best, best_ref[0:1, :])
    slot, member = iota((128, 512), 0), iota((128, 512), 1)
    spread = jnp.where(member // 4 == slot, jnp.broadcast_to(best, (128, 512)), -1.0)
    for rank in range(4):
        back_ref[:, rank : rank + 1] = jnp.max(
            jnp.where(member % 4 == rank, spread, -1.0), axis=1, keepdims=True
        )


def vmem_call(kernel, shape, name, flops, *operands):
    return pl.pallas_call(
        kernel,
        out_shape=jax.ShapeDtypeStruct(shape, F32),
        in_specs=in_vmem(len(operands)),
        out_specs=in_vmem(1)[0],
        compiler_params=pltpu.CompilerParams(vmem_limit_bytes=16 * MIB),
        cost_estimate=pl.CostEstimate(flops=flops, bytes_accessed=2 * MIB, transcendentals=0),
        name=name,
    )(*operands)


def unpack_kernel(doc_ref, back_ref, out_ref):
    pairs = doc_ref.shape[0]
    doc_rows = out_ref.shape[1]
    doc_lane = iota((pairs, doc_rows), 1)
    top = jnp.full((pairs, doc_rows), -1.0, F32)
    for rank in range(4):
        hit = doc_ref[:, rank : rank + 1] == doc_lane
        top = jnp.maximum(top, jnp.where(hit, back_ref[0:pairs, rank : rank + 1], -1.0))
    out_ref[...] = jnp.max(top, axis=0, keepdims=True)


def chip_routes():
    owners = [owner_chip(position) for position in range(64)]
    direct, passing, back = [], [], []
    low, high, swap = [], [], []
    for core in range(2):
        near, far = (4, 12) if core == 0 else (1, 3)
        direct.append([chip * 2 + core for chip in owners])
        passing.append([(chip ^ near) * 2 + core for chip in owners])
        back.append(direct[-1] + passing[-1])
        for chip in range(128):
            low.append(((chip ^ near) * 2 + core, chip * 2 + core))
            high.append(((chip ^ far) * 2 + core, chip * 2 + core))
            swap.append((chip * 2 + core, chip * 2 + 1 - core))
    return direct + passing, back, low, high, swap


def body(embeddings, block_ids, block_counts):
    doc_rows = embeddings.shape[0]
    send_groups, back_groups, low_route, high_route, swap = chip_routes()
    counts = block_counts.reshape(1, -1)
    packed, docs = pack(embeddings, block_ids, counts)
    direct = lax.all_to_all(
        packed, BOTH, split_axis=0, concat_axis=0, axis_index_groups=send_groups, tiled=True
    )
    high = lax.ppermute(direct[LOW:], BOTH, high_route)
    low = lax.ppermute(direct[:LOW], BOTH, low_route)
    late_ids, late_counts, direct = lax.optimization_barrier((block_ids, counts, direct))
    row, col = labels(late_ids, late_counts)
    direct_other = lax.ppermute(direct, BOTH, swap)
    best = vmem_call(
        direct_kernel, (8, 256), "score_direct", 10**9, row, col, direct, direct_other
    )
    low, high, best = lax.optimization_barrier((low, high, best))
    low_other = lax.ppermute(low, BOTH, swap)
    high_other = lax.ppermute(high, BOTH, swap)
    best = vmem_call(
        passed_kernel, (8, 512), "score_passed", 10**9,
        row, col, direct, direct_other, low, high, best,
    )
    best = vmem_call(
        final_kernel, (128, 4), "score_final", 10**9,
        row, col, direct, low, high, low_other, high_other, best,
    )
    back = lax.all_to_all(
        best, BOTH, split_axis=0, concat_axis=0, axis_index_groups=back_groups, tiled=True
    )
    out = pl.pallas_call(
        unpack_kernel,
        out_shape=jax.ShapeDtypeStruct((1, doc_rows), F32),
        in_specs=in_vmem(2),
        out_specs=in_vmem(1)[0],
        compiler_params=pltpu.CompilerParams(vmem_limit_bytes=4 * MIB),
        name="unpack",
    )(docs, back)
    return out.reshape(doc_rows)


def solution(mesh):
    in_specs = (P(("dp", "pair"), None), P(), P())
    out_specs = P(("dp", "pair"))
    return jax.shard_map(body, mesh=mesh, in_specs=in_specs, out_specs=out_specs, check_vma=False)
```

```python
from functools import partial

import jax
import jax.numpy as jnp
from jax import lax
from jax.experimental import pallas as pl
from jax.experimental.pallas import tpu as pltpu
from jax.sharding import PartitionSpec as P

BF16 = jnp.bfloat16
F32 = jnp.float32
I32 = jnp.int32
MIB = 1024 * 1024
BOTH = ("dp", "pair")
FIRST = 37
LOW = 28


def iota(shape, dim):
    return lax.broadcasted_iota(I32, shape, dim)


def in_vmem(count):
    return [pl.BlockSpec(memory_space=pltpu.VMEM)] * count


def my_place():
    return lax.axis_index("dp").astype(I32), lax.axis_index("pair").astype(I32)


def chip_parity(chip):
    return ((chip >> 4) + (chip >> 2) + chip) & 1


def chip_position(chip):
    return chip >> 1


def listed(place):
    return (place + FIRST) & 63


def owner_chip(position):
    return 2 * position + (((position >> 3) + (position >> 1)) & 1)


def merge_twos(a, b):
    low, high = jnp.minimum(a[0], b[0]), jnp.maximum(a[1], b[1])
    return [
        jnp.maximum(a[0], b[0]), jnp.maximum(low, high), jnp.minimum(low, high), jnp.minimum(a[1], b[1])
    ]


def top_four(a, b):
    c = [jnp.maximum(x, y) for x, y in zip(a, b[::-1])]
    e, f = jnp.maximum(c[0], c[2]), jnp.maximum(c[1], c[3])
    g, h = jnp.minimum(c[0], c[2]), jnp.minimum(c[1], c[3])
    return [jnp.maximum(e, f), jnp.minimum(e, f), jnp.maximum(g, h), jnp.minimum(g, h)]


def pack_kernel(
    emb_hbm, ids_hbm, counts_hbm, packed_ref, doc_ref, emb_ref, ids_ref, counts_ref, sems
):
    copies = [
        pltpu.make_async_copy(counts_hbm, counts_ref, sems.at[0]),
        pltpu.make_async_copy(ids_hbm, ids_ref, sems.at[1]),
        pltpu.make_async_copy(emb_hbm, emb_ref, sems.at[2]),
    ]
    for copy in copies:
        copy.start()
    doc_rows = emb_ref.shape[0]
    clusters = ids_ref.shape[0] // 8
    doc_total = doc_rows * 2 * clusters
    chip, core = my_place()
    first = (chip * 2 + core) * doc_rows
    near_pair = chip_position(chip) ^ jnp.where(core == 0, 2, 0)
    turned = (chip_parity(chip) == 1) & (((near_pair - FIRST) & 63) >= LOW)
    flip = jnp.where(turned, jnp.where(core == 0, 4, 1), 0)
    diagonal = iota((clusters, clusters), 0) == iota((clusters, clusters), 1)
    even = iota((clusters, 1), 0) % 2 == 0
    lift = jnp.where(even, doc_rows, 0)
    even_wide = iota((clusters, 128), 0) % 2 == 0
    copies[0].wait()
    counts = jnp.sum(
        jnp.where(diagonal, jnp.broadcast_to(counts_ref[...], (clusters, clusters)), 0),
        axis=1,
        keepdims=True,
    )
    copies[1].wait()
    tiles = []
    for tile in range(8):
        ids = ids_ref[pl.ds(tile, clusters, stride=8), :]
        local = ids - first
        mine = (local >= 0) & (local < doc_rows) & (tile % 2 < counts) & (ids < doc_total)
        tiles.append(jnp.where(mine, local + lift, -1).astype(F32))
    twos = [(jnp.maximum(a, b), jnp.minimum(a, b)) for a, b in zip(tiles[::2], tiles[1::2])]
    fours = [merge_twos(a, b) for a, b in zip(twos[::2], twos[1::2])]
    mine_top = top_four(*fours)
    partner_top = [
        jnp.where(even_wide, pltpu.roll(a, clusters - 1, 0), pltpu.roll(a, 1, 0)) for a in mine_top
    ]
    ranked = top_four(mine_top, partner_top)
    ranked = [jnp.transpose(a) for a in ranked]
    doc_column = iota((doc_rows, clusters), 0).astype(F32)
    which = iota((clusters, clusters), 0)
    picked = jnp.zeros((clusters, clusters), F32)
    hits = []
    for rank in range(4):
        top = jnp.max(ranked[0], axis=0, keepdims=True)
        hit = ranked[0] == top
        ranked = [jnp.where(hit, b, a) for a, b in zip(ranked, ranked[1:])]
        doc = jnp.where(top >= doc_rows, top - doc_rows, top)
        picked = jnp.where(which == rank, doc, picked)
        hits.append((doc == doc_column).astype(BF16))
    pairs = clusters // 2
    rows = 4 * pairs
    row, spot = iota((rows, 4 * clusters), 0), iota((rows, 4 * clusters), 1)
    spread = (spot == (row & 3) * clusters + 2 * (listed(row >> 2) ^ flip)).astype(BF16)
    last = (((1,), (1,)), ((), ()))
    pick = lax.dot_general(
        spread, jnp.concatenate(hits, axis=1), last, preferred_element_type=F32
    ).astype(BF16)
    take_pair = iota((pairs, clusters), 1) == 2 * listed(iota((pairs, clusters), 0))
    doc_ref[...] = lax.dot_general(
        take_pair.astype(BF16), picked.astype(BF16), last, preferred_element_type=F32
    ).astype(I32)
    copies[2].wait()
    emb = emb_ref[...]
    square = jnp.sum(emb * emb, axis=1, keepdims=True)
    normed = (emb * lax.rsqrt(square + 1e-06)).astype(BF16)
    packed = jnp.dot(pick, normed, preferred_element_type=F32).astype(BF16)
    packed_ref[...] = packed.reshape(packed_ref.shape)


def in_hbm(array):
    return pltpu.with_memory_space_constraint(array, pltpu.HBM)


def pack(embeddings, block_ids, counts):
    clusters, blocks, block_rows = block_ids.shape
    tiles = block_rows // 128
    block_ids = block_ids.reshape(clusters, blocks, tiles, 128).transpose(0, 2, 1, 3)
    block_ids = block_ids.reshape(clusters * tiles * blocks, 128)
    embeddings, block_ids, counts = in_hbm(embeddings), in_hbm(block_ids), in_hbm(counts)
    doc_rows, feature = embeddings.shape
    return pl.pallas_call(
        pack_kernel,
        out_shape=(
            jax.ShapeDtypeStruct((clusters // 2, 4, feature), BF16),
            jax.ShapeDtypeStruct((clusters // 2, 128), I32),
        ),
        in_specs=[pl.BlockSpec(memory_space=pltpu.HBM)] * 3,
        out_specs=tuple(in_vmem(2)),
        scratch_shapes=[
            pltpu.VMEM(embeddings.shape, F32),
            pltpu.VMEM(block_ids.shape, I32),
            pltpu.VMEM(counts.shape, I32),
            pltpu.SemaphoreType.DMA((3,)),
        ],
        compiler_params=pltpu.CompilerParams(vmem_limit_bytes=24 * MIB),
        name="pack",
    )(embeddings, block_ids, counts)


def label_kernel(ids_hbm, counts_hbm, row_ref, col_ref, ids_ref, counts_ref, sems):
    blocks, block_rows = ids_ref.shape
    chip, core = my_place()
    cluster = 2 * chip_position(chip)
    ids_copy = pltpu.make_async_copy(ids_hbm.at[cluster], ids_ref, sems.at[0])
    counts_copy = pltpu.make_async_copy(counts_hbm, counts_ref, sems.at[1])
    ids_copy.start()
    counts_copy.start()
    group = iota((256, 1), 0)
    of_core = jnp.where(group < 128, core, 1 - core)
    hop = jnp.where(of_core == 0, 4, 1)
    base = owner_chip(listed(group & 63))
    source = jnp.where((group & 64) == 0, base, base ^ hop) * 2 + of_core
    counts_copy.wait()
    counts = counts_ref[...]
    count = jnp.sum(jnp.where(iota(counts.shape, 1) == cluster, counts, 0), axis=1, keepdims=True)
    ids_copy.wait()
    hits = jnp.zeros((256, block_rows), F32)
    for block in range(blocks):
        ids = ids_ref[block : block + 1, :]
        slot_source = jnp.where(block < count, ids >> 8, -1)
        hits = hits + jnp.where(source == slot_source, 1.0, 0.0)
    tally = jnp.sum(hits, axis=1, keepdims=True)
    tally_wide = jnp.broadcast_to(tally, (256, 128)).astype(BF16)
    col_spread = (iota((1024, 256), 0) // 4 == iota((1024, 256), 1)).astype(BF16)
    by_row = jnp.dot(col_spread, tally_wide, preferred_element_type=F32)
    rank = (iota((1024, 128), 0) % 4).astype(F32)
    col = jnp.where(rank >= by_row, 1.0, 0.0)
    col_ref[...] = col
    row_ref[...] = jnp.transpose(col[:512])[:8]


def labels(block_ids, counts):
    block_ids, counts = in_hbm(block_ids), in_hbm(counts)
    return pl.pallas_call(
        label_kernel,
        out_shape=(
            jax.ShapeDtypeStruct((8, 512), F32),
            jax.ShapeDtypeStruct((1024, 128), F32),
        ),
        in_specs=[pl.BlockSpec(memory_space=pltpu.HBM)] * 2,
        out_specs=tuple(in_vmem(2)),
        scratch_shapes=[
            pltpu.VMEM(block_ids.shape[1:], I32),
            pltpu.VMEM(counts.shape, I32),
            pltpu.SemaphoreType.DMA((2,)),
        ],
        compiler_params=pltpu.CompilerParams(vmem_limit_bytes=16 * MIB),
        cost_estimate=pl.CostEstimate(flops=10**9, bytes_accessed=4 * MIB, transcendentals=0),
        name="labels",
    )(block_ids, counts)


def column_best(others, own, other_label, own_label, offset=None):
    scores = lax.dot_general(others, own, (((1,), (1,)), ((), ())), preferred_element_type=F32)
    same = other_label == own_label
    if offset is not None:
        same = same & (iota(scores.shape, 0) + offset != iota(scores.shape, 1))
    return jnp.max(jnp.where(same, scores, -1.0), axis=0, keepdims=True)


def rows_of(*refs):
    rows = [ref[...].reshape(4 * ref.shape[0], ref.shape[2]) for ref in refs]
    return rows[0] if len(rows) == 1 else jnp.concatenate(rows, axis=0)


def direct_kernel(row_ref, col_ref, direct_ref, best_ref):
    own = rows_of(direct_ref)
    best = column_best(own, own, col_ref[0:256, 0:1], row_ref[0:1, 0:256], 0)
    best_ref[...] = jnp.broadcast_to(best, best_ref.shape)


def passed_kernel(
    row_ref, col_ref, direct_ref, direct_other_ref, low_ref, high_ref, best_direct_ref, best_ref
):
    direct, passed = rows_of(direct_ref), rows_of(low_ref, high_ref)
    own = jnp.concatenate([direct, passed], axis=0)
    best = jnp.maximum(
        column_best(passed, own, col_ref[256:512, 0:1], row_ref[0:1, :], 256),
        column_best(rows_of(direct_other_ref), own, col_ref[512:768, 0:1], row_ref[0:1, :]),
    )
    best_passed = column_best(direct, passed, col_ref[0:256, 0:1], row_ref[0:1, 256:512])
    best = jnp.maximum(
        best, jnp.concatenate([best_direct_ref[0:1, :], best_passed], axis=1)
    )
    best_ref[...] = jnp.broadcast_to(best, best_ref.shape)


def final_kernel(
    row_ref, col_ref, direct_ref, low_ref, high_ref, low_other_ref, high_other_ref, best_ref, back_ref
):
    own = rows_of(direct_ref, low_ref, high_ref)
    others = rows_of(low_other_ref, high_other_ref)
    best = column_best(others, own, col_ref[768:1024, 0:1], row_ref[0:1, :])
    best = jnp.maximum(best, best_ref[0:1, :])
    slot, member = iota((128, 512), 0), iota((128, 512), 1)
    spread = jnp.where(member // 4 == slot, jnp.broadcast_to(best, (128, 512)), -1.0)
    for rank in range(4):
        back_ref[:, rank : rank + 1] = jnp.max(
            jnp.where(member % 4 == rank, spread, -1.0), axis=1, keepdims=True
        )


def vmem_call(kernel, shape, name, flops, *operands):
    return pl.pallas_call(
        kernel,
        out_shape=jax.ShapeDtypeStruct(shape, F32),
        in_specs=in_vmem(len(operands)),
        out_specs=in_vmem(1)[0],
        compiler_params=pltpu.CompilerParams(vmem_limit_bytes=16 * MIB),
        cost_estimate=pl.CostEstimate(flops=flops, bytes_accessed=2 * MIB, transcendentals=0),
        name=name,
    )(*operands)


def unpack_kernel(doc_ref, back_ref, out_ref):
    pairs = doc_ref.shape[0]
    doc_rows = out_ref.shape[1]
    doc_lane = iota((pairs, doc_rows), 1)
    top = jnp.full((pairs, doc_rows), -1.0, F32)
    for rank in range(4):
        hit = doc_ref[:, rank : rank + 1] == doc_lane
        top = jnp.maximum(top, jnp.where(hit, back_ref[0:pairs, rank : rank + 1], -1.0))
    out_ref[...] = jnp.max(top, axis=0, keepdims=True)


def chip_routes():
    owners = [owner_chip(listed(place)) for place in range(64)]
    direct, passing, back = [], [], []
    low, high, swap = [], [], []
    for core in range(2):
        near, far = (4, 12) if core == 0 else (1, 3)
        direct.append([chip * 2 + core for chip in owners])
        passing.append([(chip ^ near) * 2 + core for chip in owners])
        back.append(direct[-1] + passing[-1])
        for chip in range(128):
            low.append(((chip ^ near) * 2 + core, chip * 2 + core))
            high.append(((chip ^ far) * 2 + core, chip * 2 + core))
            swap.append((chip * 2 + core, chip * 2 + 1 - core))
    return direct + passing, back, low, high, swap


def body(embeddings, block_ids, block_counts):
    doc_rows = embeddings.shape[0]
    send_groups, back_groups, low_route, high_route, swap = chip_routes()
    counts = block_counts.reshape(1, -1)
    packed, docs = pack(embeddings, block_ids, counts)
    direct = lax.all_to_all(
        packed, BOTH, split_axis=0, concat_axis=0, axis_index_groups=send_groups, tiled=True
    )
    high = lax.ppermute(direct[LOW:], BOTH, high_route)
    low = lax.ppermute(direct[:LOW], BOTH, low_route)
    late_ids, late_counts, direct = lax.optimization_barrier((block_ids, counts, direct))
    row, col = labels(late_ids, late_counts)
    direct_other = lax.ppermute(direct, BOTH, swap)
    best = vmem_call(direct_kernel, (8, 256), "score_direct", 10**9, row, col, direct)
    low, best = lax.optimization_barrier((low, best))
    low_other = lax.ppermute(low, BOTH, swap)
    high, best = lax.optimization_barrier((high, best))
    high_other = lax.ppermute(high, BOTH, swap)
    best = vmem_call(
        passed_kernel, (8, 512), "score_passed", 10**9,
        row, col, direct, direct_other, low, high, best,
    )
    best = vmem_call(
        final_kernel, (128, 4), "score_final", 10**9,
        row, col, direct, low, high, low_other, high_other, best,
    )
    back = lax.all_to_all(
        best, BOTH, split_axis=0, concat_axis=0, axis_index_groups=back_groups, tiled=True
    )
    out = pl.pallas_call(
        unpack_kernel,
        out_shape=jax.ShapeDtypeStruct((1, doc_rows), F32),
        in_specs=in_vmem(2),
        out_specs=in_vmem(1)[0],
        compiler_params=pltpu.CompilerParams(vmem_limit_bytes=4 * MIB),
        name="unpack",
    )(docs, back)
    return out.reshape(doc_rows)


def solution(mesh):
    in_specs = (P(("dp", "pair"), None), P(), P())
    out_specs = P(("dp", "pair"))
    return jax.shard_map(body, mesh=mesh, in_specs=in_specs, out_specs=out_specs, check_vma=False)
```

```python
from functools import partial

import jax
import jax.numpy as jnp
from jax import lax
from jax.experimental import pallas as pl
from jax.experimental.pallas import tpu as pltpu
from jax.sharding import PartitionSpec as P

BF16 = jnp.bfloat16
F32 = jnp.float32
I32 = jnp.int32
MIB = 1024 * 1024
BOTH = ("dp", "pair")
FIRST = 37
LOW = 32


def iota(shape, dim):
    return lax.broadcasted_iota(I32, shape, dim)


def in_vmem(count):
    return [pl.BlockSpec(memory_space=pltpu.VMEM)] * count


def my_place():
    return lax.axis_index("dp").astype(I32), lax.axis_index("pair").astype(I32)


def chip_parity(chip):
    return ((chip >> 4) + (chip >> 2) + chip) & 1


def chip_position(chip):
    return chip >> 1


def listed(place):
    return (place + FIRST) & 63


def owner_chip(position):
    return 2 * position + (((position >> 3) + (position >> 1)) & 1)


def merge_twos(a, b):
    low, high = jnp.minimum(a[0], b[0]), jnp.maximum(a[1], b[1])
    return [
        jnp.maximum(a[0], b[0]), jnp.maximum(low, high), jnp.minimum(low, high), jnp.minimum(a[1], b[1])
    ]


def top_four(a, b):
    c = [jnp.maximum(x, y) for x, y in zip(a, b[::-1])]
    e, f = jnp.maximum(c[0], c[2]), jnp.maximum(c[1], c[3])
    g, h = jnp.minimum(c[0], c[2]), jnp.minimum(c[1], c[3])
    return [jnp.maximum(e, f), jnp.minimum(e, f), jnp.maximum(g, h), jnp.minimum(g, h)]


def pack_kernel(
    emb_hbm, ids_hbm, counts_hbm, packed_ref, doc_ref, emb_ref, ids_ref, counts_ref, sems
):
    copies = [
        pltpu.make_async_copy(counts_hbm, counts_ref, sems.at[0]),
        pltpu.make_async_copy(ids_hbm, ids_ref, sems.at[1]),
        pltpu.make_async_copy(emb_hbm, emb_ref, sems.at[2]),
    ]
    for copy in copies:
        copy.start()
    doc_rows = emb_ref.shape[0]
    clusters = ids_ref.shape[0] // 8
    doc_total = doc_rows * 2 * clusters
    chip, core = my_place()
    first = (chip * 2 + core) * doc_rows
    near_pair = chip_position(chip) ^ jnp.where(core == 0, 2, 0)
    turned = (chip_parity(chip) == 1) & (((near_pair - FIRST) & 63) >= LOW)
    flip = jnp.where(turned, jnp.where(core == 0, 10, 1), 0)
    diagonal = iota((clusters, clusters), 0) == iota((clusters, clusters), 1)
    even = iota((clusters, 1), 0) % 2 == 0
    lift = jnp.where(even, doc_rows, 0)
    even_wide = iota((clusters, 128), 0) % 2 == 0
    copies[0].wait()
    counts = jnp.sum(
        jnp.where(diagonal, jnp.broadcast_to(counts_ref[...], (clusters, clusters)), 0),
        axis=1,
        keepdims=True,
    )
    copies[1].wait()
    tiles = []
    for tile in range(8):
        ids = ids_ref[pl.ds(tile, clusters, stride=8), :]
        local = ids - first
        mine = (local >= 0) & (local < doc_rows) & (tile % 2 < counts) & (ids < doc_total)
        tiles.append(jnp.where(mine, local + lift, -1).astype(F32))
    twos = [(jnp.maximum(a, b), jnp.minimum(a, b)) for a, b in zip(tiles[::2], tiles[1::2])]
    fours = [merge_twos(a, b) for a, b in zip(twos[::2], twos[1::2])]
    mine_top = top_four(*fours)
    partner_top = [
        jnp.where(even_wide, pltpu.roll(a, clusters - 1, 0), pltpu.roll(a, 1, 0)) for a in mine_top
    ]
    ranked = top_four(mine_top, partner_top)
    ranked = [jnp.transpose(a) for a in ranked]
    doc_column = iota((doc_rows, clusters), 0).astype(F32)
    which = iota((clusters, clusters), 0)
    picked = jnp.zeros((clusters, clusters), F32)
    hits = []
    for rank in range(4):
        top = jnp.max(ranked[0], axis=0, keepdims=True)
        hit = ranked[0] == top
        ranked = [jnp.where(hit, b, a) for a, b in zip(ranked, ranked[1:])]
        doc = jnp.where(top >= doc_rows, top - doc_rows, top)
        picked = jnp.where(which == rank, doc, picked)
        hits.append((doc == doc_column).astype(BF16))
    pairs = clusters // 2
    rows = 4 * pairs
    row, spot = iota((rows, 4 * clusters), 0), iota((rows, 4 * clusters), 1)
    spread = (spot == (row & 3) * clusters + 2 * (listed(row >> 2) ^ flip)).astype(BF16)
    last = (((1,), (1,)), ((), ()))
    pick = lax.dot_general(
        spread, jnp.concatenate(hits, axis=1), last, preferred_element_type=F32
    ).astype(BF16)
    take_pair = iota((pairs, clusters), 1) == 2 * listed(iota((pairs, clusters), 0))
    doc_ref[...] = lax.dot_general(
        take_pair.astype(BF16), picked.astype(BF16), last, preferred_element_type=F32
    ).astype(I32)
    copies[2].wait()
    emb = emb_ref[...]
    square = jnp.sum(emb * emb, axis=1, keepdims=True)
    normed = (emb * lax.rsqrt(square + 1e-06)).astype(BF16)
    packed = jnp.dot(pick, normed, preferred_element_type=F32).astype(BF16)
    packed_ref[...] = packed.reshape(packed_ref.shape)


def in_hbm(array):
    return pltpu.with_memory_space_constraint(array, pltpu.HBM)


def pack(embeddings, block_ids, counts):
    clusters, blocks, block_rows = block_ids.shape
    tiles = block_rows // 128
    block_ids = block_ids.reshape(clusters, blocks, tiles, 128).transpose(0, 2, 1, 3)
    block_ids = block_ids.reshape(clusters * tiles * blocks, 128)
    embeddings, block_ids, counts = in_hbm(embeddings), in_hbm(block_ids), in_hbm(counts)
    doc_rows, feature = embeddings.shape
    return pl.pallas_call(
        pack_kernel,
        out_shape=(
            jax.ShapeDtypeStruct((clusters // 2, 4, feature), BF16),
            jax.ShapeDtypeStruct((clusters // 2, 128), I32),
        ),
        in_specs=[pl.BlockSpec(memory_space=pltpu.HBM)] * 3,
        out_specs=tuple(in_vmem(2)),
        scratch_shapes=[
            pltpu.VMEM(embeddings.shape, F32),
            pltpu.VMEM(block_ids.shape, I32),
            pltpu.VMEM(counts.shape, I32),
            pltpu.SemaphoreType.DMA((3,)),
        ],
        compiler_params=pltpu.CompilerParams(vmem_limit_bytes=24 * MIB),
        name="pack",
    )(embeddings, block_ids, counts)


def label_kernel(ids_hbm, counts_hbm, row_ref, col_ref, ids_ref, counts_ref, sems):
    blocks, block_rows = ids_ref.shape
    chip, core = my_place()
    cluster = 2 * chip_position(chip)
    ids_copy = pltpu.make_async_copy(ids_hbm.at[cluster], ids_ref, sems.at[0])
    counts_copy = pltpu.make_async_copy(counts_hbm, counts_ref, sems.at[1])
    ids_copy.start()
    counts_copy.start()
    group = iota((256, 1), 0)
    of_core = jnp.where(group < 128, core, 1 - core)
    hop = jnp.where(of_core == 0, 4, 1)
    base = owner_chip(listed(group & 63))
    source = jnp.where((group & 64) == 0, base, base ^ hop) * 2 + of_core
    counts_copy.wait()
    counts = counts_ref[...]
    count = jnp.sum(jnp.where(iota(counts.shape, 1) == cluster, counts, 0), axis=1, keepdims=True)
    ids_copy.wait()
    hits = jnp.zeros((256, block_rows), F32)
    for block in range(blocks):
        ids = ids_ref[block : block + 1, :]
        slot_source = jnp.where(block < count, ids >> 8, -1)
        hits = hits + jnp.where(source == slot_source, 1.0, 0.0)
    tally = jnp.sum(hits, axis=1, keepdims=True)
    tally_wide = jnp.broadcast_to(tally, (256, 128)).astype(BF16)
    col_spread = (iota((1024, 256), 0) // 4 == iota((1024, 256), 1)).astype(BF16)
    by_row = jnp.dot(col_spread, tally_wide, preferred_element_type=F32)
    rank = (iota((1024, 128), 0) % 4).astype(F32)
    col = jnp.where(rank >= by_row, 1.0, 0.0)
    col_ref[...] = col
    row_ref[...] = jnp.transpose(col[:512])[:8]


def labels(block_ids, counts):
    block_ids, counts = in_hbm(block_ids), in_hbm(counts)
    return pl.pallas_call(
        label_kernel,
        out_shape=(
            jax.ShapeDtypeStruct((8, 512), F32),
            jax.ShapeDtypeStruct((1024, 128), F32),
        ),
        in_specs=[pl.BlockSpec(memory_space=pltpu.HBM)] * 2,
        out_specs=tuple(in_vmem(2)),
        scratch_shapes=[
            pltpu.VMEM(block_ids.shape[1:], I32),
            pltpu.VMEM(counts.shape, I32),
            pltpu.SemaphoreType.DMA((2,)),
        ],
        compiler_params=pltpu.CompilerParams(vmem_limit_bytes=16 * MIB),
        cost_estimate=pl.CostEstimate(flops=10**9, bytes_accessed=4 * MIB, transcendentals=0),
        name="labels",
    )(block_ids, counts)


def column_best(others, own, other_label, own_label, offset=None):
    scores = lax.dot_general(others, own, (((1,), (1,)), ((), ())), preferred_element_type=F32)
    same = other_label == own_label
    if offset is not None:
        same = same & (iota(scores.shape, 0) + offset != iota(scores.shape, 1))
    return jnp.max(jnp.where(same, scores, -1.0), axis=0, keepdims=True)


def rows_of(*refs):
    rows = [ref[...].reshape(4 * ref.shape[0], ref.shape[2]) for ref in refs]
    return rows[0] if len(rows) == 1 else jnp.concatenate(rows, axis=0)


def direct_kernel(row_ref, col_ref, direct_ref, best_ref):
    own = rows_of(direct_ref)
    best = column_best(own, own, col_ref[0:256, 0:1], row_ref[0:1, 0:256], 0)
    best_ref[...] = jnp.broadcast_to(best, best_ref.shape)


def passed_kernel(
    row_ref, col_ref, direct_ref, direct_other_ref, low_ref, high_ref, best_direct_ref, best_ref
):
    direct, passed = rows_of(direct_ref), rows_of(low_ref, high_ref)
    own = jnp.concatenate([direct, passed], axis=0)
    best = jnp.maximum(
        column_best(passed, own, col_ref[256:512, 0:1], row_ref[0:1, :], 256),
        column_best(rows_of(direct_other_ref), own, col_ref[512:768, 0:1], row_ref[0:1, :]),
    )
    best_passed = column_best(direct, passed, col_ref[0:256, 0:1], row_ref[0:1, 256:512])
    best = jnp.maximum(
        best, jnp.concatenate([best_direct_ref[0:1, :], best_passed], axis=1)
    )
    best_ref[...] = jnp.broadcast_to(best, best_ref.shape)


def final_kernel(
    row_ref, col_ref, direct_ref, low_ref, high_ref, low_other_ref, high_other_ref, best_ref, back_ref
):
    own = rows_of(direct_ref, low_ref, high_ref)
    others = rows_of(low_other_ref, high_other_ref)
    best = column_best(others, own, col_ref[768:1024, 0:1], row_ref[0:1, :])
    best = jnp.maximum(best, best_ref[0:1, :])
    slot, member = iota((128, 512), 0), iota((128, 512), 1)
    spread = jnp.where(member // 4 == slot, jnp.broadcast_to(best, (128, 512)), -1.0)
    for rank in range(4):
        back_ref[:, rank : rank + 1] = jnp.max(
            jnp.where(member % 4 == rank, spread, -1.0), axis=1, keepdims=True
        )


def vmem_call(kernel, shape, name, flops, *operands):
    return pl.pallas_call(
        kernel,
        out_shape=jax.ShapeDtypeStruct(shape, F32),
        in_specs=in_vmem(len(operands)),
        out_specs=in_vmem(1)[0],
        compiler_params=pltpu.CompilerParams(vmem_limit_bytes=16 * MIB),
        cost_estimate=pl.CostEstimate(flops=flops, bytes_accessed=2 * MIB, transcendentals=0),
        name=name,
    )(*operands)


def unpack_kernel(doc_ref, back_ref, out_ref):
    pairs = doc_ref.shape[0]
    doc_rows = out_ref.shape[1]
    doc_lane = iota((pairs, doc_rows), 1)
    top = jnp.full((pairs, doc_rows), -1.0, F32)
    for rank in range(4):
        hit = doc_ref[:, rank : rank + 1] == doc_lane
        top = jnp.maximum(top, jnp.where(hit, back_ref[0:pairs, rank : rank + 1], -1.0))
    out_ref[...] = jnp.max(top, axis=0, keepdims=True)


def chip_routes():
    owners = [owner_chip(listed(place)) for place in range(64)]
    direct, passing, back = [], [], []
    low, high, swap = [], [], []
    for core in range(2):
        near, far = (4, 16) if core == 0 else (1, 3)
        direct.append([chip * 2 + core for chip in owners])
        passing.append([(chip ^ near) * 2 + core for chip in owners])
        back.append(direct[-1] + passing[-1])
        for chip in range(128):
            low.append(((chip ^ near) * 2 + core, chip * 2 + core))
            high.append(((chip ^ far) * 2 + core, chip * 2 + core))
            swap.append((chip * 2 + core, chip * 2 + 1 - core))
    return direct + passing, back, low, high, swap


def body(embeddings, block_ids, block_counts):
    doc_rows = embeddings.shape[0]
    send_groups, back_groups, low_route, high_route, swap = chip_routes()
    counts = block_counts.reshape(1, -1)
    packed, docs = pack(embeddings, block_ids, counts)
    direct = lax.all_to_all(
        packed, BOTH, split_axis=0, concat_axis=0, axis_index_groups=send_groups, tiled=True
    )
    high = lax.ppermute(direct[LOW:], BOTH, high_route)
    low = lax.ppermute(direct[:LOW], BOTH, low_route)
    late_ids, late_counts, direct = lax.optimization_barrier((block_ids, counts, direct))
    row, col = labels(late_ids, late_counts)
    direct_other = lax.ppermute(direct, BOTH, swap)
    best = vmem_call(direct_kernel, (8, 256), "score_direct", 10**9, row, col, direct)
    low, best = lax.optimization_barrier((low, best))
    low_other = lax.ppermute(low, BOTH, swap)
    high, best = lax.optimization_barrier((high, best))
    high_other = lax.ppermute(high, BOTH, swap)
    best = vmem_call(
        passed_kernel, (8, 512), "score_passed", 10**9,
        row, col, direct, direct_other, low, high, best,
    )
    best = vmem_call(
        final_kernel, (128, 4), "score_final", 10**9,
        row, col, direct, low, high, low_other, high_other, best,
    )
    back = lax.all_to_all(
        best, BOTH, split_axis=0, concat_axis=0, axis_index_groups=back_groups, tiled=True
    )
    out = pl.pallas_call(
        unpack_kernel,
        out_shape=jax.ShapeDtypeStruct((1, doc_rows), F32),
        in_specs=in_vmem(2),
        out_specs=in_vmem(1)[0],
        compiler_params=pltpu.CompilerParams(vmem_limit_bytes=4 * MIB),
        name="unpack",
    )(docs, back)
    return out.reshape(doc_rows)


def solution(mesh):
    in_specs = (P(("dp", "pair"), None), P(), P())
    out_specs = P(("dp", "pair"))
    return jax.shard_map(body, mesh=mesh, in_specs=in_specs, out_specs=out_specs, check_vma=False)
```

```python
from functools import partial

import jax
import jax.numpy as jnp
from jax import lax
from jax.experimental import pallas as pl
from jax.experimental.pallas import tpu as pltpu
from jax.sharding import PartitionSpec as P

BF16 = jnp.bfloat16
F32 = jnp.float32
I32 = jnp.int32
MIB = 1024 * 1024
BOTH = ("dp", "pair")
FIRST = 37
LOW = 32


def iota(shape, dim):
    return lax.broadcasted_iota(I32, shape, dim)


def in_vmem(count):
    return [pl.BlockSpec(memory_space=pltpu.VMEM)] * count


def my_place():
    return lax.axis_index("dp").astype(I32), lax.axis_index("pair").astype(I32)


def chip_parity(chip):
    return ((chip >> 4) + (chip >> 2) + chip) & 1


def chip_position(chip):
    return chip >> 1


def listed(place):
    return (place + FIRST) & 63


def owner_chip(position):
    return 2 * position + (((position >> 3) + (position >> 1)) & 1)


def merge_twos(a, b):
    low, high = jnp.minimum(a[0], b[0]), jnp.maximum(a[1], b[1])
    return [
        jnp.maximum(a[0], b[0]), jnp.maximum(low, high), jnp.minimum(low, high), jnp.minimum(a[1], b[1])
    ]


def top_four(a, b):
    c = [jnp.maximum(x, y) for x, y in zip(a, b[::-1])]
    e, f = jnp.maximum(c[0], c[2]), jnp.maximum(c[1], c[3])
    g, h = jnp.minimum(c[0], c[2]), jnp.minimum(c[1], c[3])
    return [jnp.maximum(e, f), jnp.minimum(e, f), jnp.maximum(g, h), jnp.minimum(g, h)]


def pack_kernel(
    emb_hbm, ids_hbm, counts_hbm, packed_ref, doc_ref, emb_ref, ids_ref, counts_ref, sems
):
    copies = [
        pltpu.make_async_copy(counts_hbm, counts_ref, sems.at[0]),
        pltpu.make_async_copy(ids_hbm, ids_ref, sems.at[1]),
        pltpu.make_async_copy(emb_hbm, emb_ref, sems.at[2]),
    ]
    for copy in copies:
        copy.start()
    doc_rows = emb_ref.shape[0]
    clusters = ids_ref.shape[0] // 8
    doc_total = doc_rows * 2 * clusters
    chip, core = my_place()
    first = (chip * 2 + core) * doc_rows
    near_pair = chip_position(chip) ^ jnp.where(core == 0, 2, 0)
    turned = (chip_parity(chip) == 1) & (((near_pair - FIRST) & 63) >= LOW)
    flip = jnp.where(turned, jnp.where(core == 0, 10, 1), 0)
    diagonal = iota((clusters, clusters), 0) == iota((clusters, clusters), 1)
    even = iota((clusters, 1), 0) % 2 == 0
    lift = jnp.where(even, doc_rows, 0)
    even_wide = iota((clusters, 128), 0) % 2 == 0
    copies[0].wait()
    counts = jnp.sum(
        jnp.where(diagonal, jnp.broadcast_to(counts_ref[...], (clusters, clusters)), 0),
        axis=1,
        keepdims=True,
    )
    copies[1].wait()
    tiles = []
    for tile in range(8):
        ids = ids_ref[pl.ds(tile, clusters, stride=8), :]
        local = ids - first
        mine = (local >= 0) & (local < doc_rows) & (tile % 2 < counts) & (ids < doc_total)
        tiles.append(jnp.where(mine, local + lift, -1).astype(F32))
    twos = [(jnp.maximum(a, b), jnp.minimum(a, b)) for a, b in zip(tiles[::2], tiles[1::2])]
    fours = [merge_twos(a, b) for a, b in zip(twos[::2], twos[1::2])]
    mine_top = top_four(*fours)
    partner_top = [
        jnp.where(even_wide, pltpu.roll(a, clusters - 1, 0), pltpu.roll(a, 1, 0)) for a in mine_top
    ]
    ranked = top_four(mine_top, partner_top)
    ranked = [jnp.transpose(a) for a in ranked]
    doc_column = iota((doc_rows, clusters), 0).astype(F32)
    which = iota((clusters, clusters), 0)
    picked = jnp.zeros((clusters, clusters), F32)
    hits = []
    for rank in range(4):
        top = jnp.max(ranked[0], axis=0, keepdims=True)
        hit = ranked[0] == top
        ranked = [jnp.where(hit, b, a) for a, b in zip(ranked, ranked[1:])]
        doc = jnp.where(top >= doc_rows, top - doc_rows, top)
        picked = jnp.where(which == rank, doc, picked)
        hits.append((doc == doc_column).astype(BF16))
    pairs = clusters // 2
    rows = 4 * pairs
    row, spot = iota((rows, 4 * clusters), 0), iota((rows, 4 * clusters), 1)
    spread = (spot == (row & 3) * clusters + 2 * (listed(row >> 2) ^ flip)).astype(BF16)
    last = (((1,), (1,)), ((), ()))
    copies[2].wait()
    pick = lax.dot_general(
        spread, jnp.concatenate(hits, axis=1), last, preferred_element_type=F32
    ).astype(BF16)
    emb = emb_ref[...]
    square = jnp.sum(emb * emb, axis=1, keepdims=True)
    normed = (emb * lax.rsqrt(square + 1e-06)).astype(BF16)
    packed = jnp.dot(pick, normed, preferred_element_type=F32).astype(BF16)
    packed_ref[...] = packed.reshape(packed_ref.shape)
    take_pair = iota((pairs, clusters), 1) == 2 * listed(iota((pairs, clusters), 0))
    doc_ref[...] = lax.dot_general(
        take_pair.astype(BF16), picked.astype(BF16), last, preferred_element_type=F32
    ).astype(I32)


def in_hbm(array):
    return pltpu.with_memory_space_constraint(array, pltpu.HBM)


def pack(embeddings, block_ids, counts):
    clusters, blocks, block_rows = block_ids.shape
    tiles = block_rows // 128
    block_ids = block_ids.reshape(clusters, blocks, tiles, 128).transpose(0, 2, 1, 3)
    block_ids = block_ids.reshape(clusters * tiles * blocks, 128)
    embeddings, block_ids, counts = in_hbm(embeddings), in_hbm(block_ids), in_hbm(counts)
    doc_rows, feature = embeddings.shape
    return pl.pallas_call(
        pack_kernel,
        out_shape=(
            jax.ShapeDtypeStruct((clusters // 2, 4, feature), BF16),
            jax.ShapeDtypeStruct((clusters // 2, 128), I32),
        ),
        in_specs=[pl.BlockSpec(memory_space=pltpu.HBM)] * 3,
        out_specs=tuple(in_vmem(2)),
        scratch_shapes=[
            pltpu.VMEM(embeddings.shape, F32),
            pltpu.VMEM(block_ids.shape, I32),
            pltpu.VMEM(counts.shape, I32),
            pltpu.SemaphoreType.DMA((3,)),
        ],
        compiler_params=pltpu.CompilerParams(vmem_limit_bytes=24 * MIB),
        name="pack",
    )(embeddings, block_ids, counts)


def label_kernel(ids_hbm, counts_hbm, row_ref, col_ref, ids_ref, counts_ref, sems):
    blocks, block_rows = ids_ref.shape
    chip, core = my_place()
    cluster = 2 * chip_position(chip)
    ids_copy = pltpu.make_async_copy(ids_hbm.at[cluster], ids_ref, sems.at[0])
    counts_copy = pltpu.make_async_copy(counts_hbm, counts_ref, sems.at[1])
    ids_copy.start()
    counts_copy.start()
    group = iota((256, 1), 0)
    of_core = jnp.where(group < 128, core, 1 - core)
    hop = jnp.where(of_core == 0, 4, 1)
    base = owner_chip(listed(group & 63))
    source = jnp.where((group & 64) == 0, base, base ^ hop) * 2 + of_core
    counts_copy.wait()
    counts = counts_ref[...]
    count = jnp.sum(jnp.where(iota(counts.shape, 1) == cluster, counts, 0), axis=1, keepdims=True)
    ids_copy.wait()
    hits = jnp.zeros((256, block_rows), F32)
    for block in range(blocks):
        ids = ids_ref[block : block + 1, :]
        slot_source = jnp.where(block < count, ids >> 8, -1)
        hits = hits + jnp.where(source == slot_source, 1.0, 0.0)
    tally = jnp.sum(hits, axis=1, keepdims=True)
    tally_wide = jnp.broadcast_to(tally, (256, 128)).astype(BF16)
    col_spread = (iota((1024, 256), 0) // 4 == iota((1024, 256), 1)).astype(BF16)
    by_row = jnp.dot(col_spread, tally_wide, preferred_element_type=F32)
    rank = (iota((1024, 128), 0) % 4).astype(F32)
    col = jnp.where(rank >= by_row, 1.0, 0.0)
    col_ref[...] = col
    row_ref[...] = jnp.transpose(col[:512])[:8]


def labels(block_ids, counts):
    block_ids, counts = in_hbm(block_ids), in_hbm(counts)
    return pl.pallas_call(
        label_kernel,
        out_shape=(
            jax.ShapeDtypeStruct((8, 512), F32),
            jax.ShapeDtypeStruct((1024, 128), F32),
        ),
        in_specs=[pl.BlockSpec(memory_space=pltpu.HBM)] * 2,
        out_specs=tuple(in_vmem(2)),
        scratch_shapes=[
            pltpu.VMEM(block_ids.shape[1:], I32),
            pltpu.VMEM(counts.shape, I32),
            pltpu.SemaphoreType.DMA((2,)),
        ],
        compiler_params=pltpu.CompilerParams(vmem_limit_bytes=16 * MIB),
        cost_estimate=pl.CostEstimate(flops=10**9, bytes_accessed=4 * MIB, transcendentals=0),
        name="labels",
    )(block_ids, counts)


def column_best(others, own, other_label, own_label, offset=None):
    scores = lax.dot_general(others, own, (((1,), (1,)), ((), ())), preferred_element_type=F32)
    same = other_label == own_label
    if offset is not None:
        same = same & (iota(scores.shape, 0) + offset != iota(scores.shape, 1))
    return jnp.max(jnp.where(same, scores, -1.0), axis=0, keepdims=True)


def rows_of(*refs):
    rows = [ref[...].reshape(4 * ref.shape[0], ref.shape[2]) for ref in refs]
    return rows[0] if len(rows) == 1 else jnp.concatenate(rows, axis=0)


def direct_kernel(row_ref, col_ref, direct_ref, best_ref):
    own = rows_of(direct_ref)
    best = column_best(own, own, col_ref[0:256, 0:1], row_ref[0:1, 0:256], 0)
    best_ref[...] = jnp.broadcast_to(best, best_ref.shape)


def low_kernel(row_ref, col_ref, direct_ref, direct_other_ref, low_ref, before_ref, best_ref):
    end = 256 + 4 * LOW
    direct, low = rows_of(direct_ref), rows_of(low_ref)
    own = jnp.concatenate([direct, low], axis=0)
    label = row_ref[0:1, 0:end]
    best = jnp.maximum(
        column_best(low, own, col_ref[256:end, 0:1], label, 256),
        column_best(rows_of(direct_other_ref), own, col_ref[512:768, 0:1], label),
    )
    best_low = column_best(direct, low, col_ref[0:256, 0:1], row_ref[0:1, 256:end])
    best = jnp.maximum(best, jnp.concatenate([before_ref[0:1, :], best_low], axis=1))
    best_ref[...] = jnp.broadcast_to(best, best_ref.shape)


def high_kernel(
    row_ref,
    col_ref,
    direct_ref,
    direct_other_ref,
    low_ref,
    low_other_ref,
    high_ref,
    before_ref,
    best_ref,
):
    start = 256 + 4 * LOW
    earlier, high = rows_of(direct_ref, low_ref), rows_of(high_ref)
    own = jnp.concatenate([earlier, high], axis=0)
    best = jnp.maximum(
        column_best(high, own, col_ref[start:512, 0:1], row_ref[0:1, :], start),
        column_best(rows_of(low_other_ref), own, col_ref[768 : start + 512, 0:1], row_ref[0:1, :]),
    )
    label = row_ref[0:1, start:512]
    best_high = jnp.maximum(
        column_best(earlier, high, col_ref[0:start, 0:1], label),
        column_best(rows_of(direct_other_ref), high, col_ref[512:768, 0:1], label),
    )
    best = jnp.maximum(best, jnp.concatenate([before_ref[0:1, :], best_high], axis=1))
    best_ref[...] = jnp.broadcast_to(best, best_ref.shape)


def final_kernel(
    row_ref, col_ref, direct_ref, low_ref, high_ref, high_other_ref, before_ref, back_ref
):
    start = 256 + 4 * LOW
    own = rows_of(direct_ref, low_ref, high_ref)
    best = column_best(
        rows_of(high_other_ref), own, col_ref[start + 512 : 1024, 0:1], row_ref[0:1, :]
    )
    best = jnp.maximum(best, before_ref[0:1, :])
    slot, member = iota((128, 512), 0), iota((128, 512), 1)
    spread = jnp.where(member // 4 == slot, jnp.broadcast_to(best, (128, 512)), -1.0)
    for rank in range(4):
        back_ref[:, rank : rank + 1] = jnp.max(
            jnp.where(member % 4 == rank, spread, -1.0), axis=1, keepdims=True
        )


def vmem_call(kernel, shape, name, flops, *operands):
    return pl.pallas_call(
        kernel,
        out_shape=jax.ShapeDtypeStruct(shape, F32),
        in_specs=in_vmem(len(operands)),
        out_specs=in_vmem(1)[0],
        compiler_params=pltpu.CompilerParams(vmem_limit_bytes=16 * MIB),
        cost_estimate=pl.CostEstimate(flops=flops, bytes_accessed=2 * MIB, transcendentals=0),
        name=name,
    )(*operands)


def unpack_kernel(doc_ref, back_ref, out_ref):
    pairs = doc_ref.shape[0]
    doc_rows = out_ref.shape[1]
    doc_lane = iota((pairs, doc_rows), 1)
    top = jnp.full((pairs, doc_rows), -1.0, F32)
    for rank in range(4):
        hit = doc_ref[:, rank : rank + 1] == doc_lane
        top = jnp.maximum(top, jnp.where(hit, back_ref[0:pairs, rank : rank + 1], -1.0))
    out_ref[...] = jnp.max(top, axis=0, keepdims=True)


def chip_routes():
    owners = [owner_chip(listed(place)) for place in range(64)]
    direct, passing, back = [], [], []
    low, high, swap = [], [], []
    for core in range(2):
        near, far = (4, 16) if core == 0 else (1, 3)
        direct.append([chip * 2 + core for chip in owners])
        passing.append([(chip ^ near) * 2 + core for chip in owners])
        back.append(direct[-1] + passing[-1])
        for chip in range(128):
            low.append(((chip ^ near) * 2 + core, chip * 2 + core))
            high.append(((chip ^ far) * 2 + core, chip * 2 + core))
            swap.append((chip * 2 + core, chip * 2 + 1 - core))
    return direct + passing, back, low, high, swap


def body(embeddings, block_ids, block_counts):
    doc_rows = embeddings.shape[0]
    send_groups, back_groups, low_route, high_route, swap = chip_routes()
    counts = block_counts.reshape(1, -1)
    packed, docs = pack(embeddings, block_ids, counts)
    direct = lax.all_to_all(
        packed, BOTH, split_axis=0, concat_axis=0, axis_index_groups=send_groups, tiled=True
    )
    high = lax.ppermute(direct[LOW:], BOTH, high_route)
    low = lax.ppermute(direct[:LOW], BOTH, low_route)
    late_ids, late_counts, direct = lax.optimization_barrier((block_ids, counts, direct))
    row, col = labels(late_ids, late_counts)
    direct_other = lax.ppermute(direct, BOTH, swap)
    best = vmem_call(direct_kernel, (8, 256), "score_direct", 10**9, row, col, direct)
    low_other = lax.ppermute(low, BOTH, swap)
    best = vmem_call(
        low_kernel, (8, 256 + 4 * LOW), "score_low", 10**9,
        row, col, direct, direct_other, low, best,
    )
    high, best = lax.optimization_barrier((high, best))
    high_other = lax.ppermute(high, BOTH, swap)
    best = vmem_call(
        high_kernel, (8, 512), "score_high", 10**9,
        row, col, direct, direct_other, low, low_other, high, best,
    )
    best = vmem_call(
        final_kernel, (128, 4), "score_final", 10**9,
        row, col, direct, low, high, high_other, best,
    )
    back = lax.all_to_all(
        best, BOTH, split_axis=0, concat_axis=0, axis_index_groups=back_groups, tiled=True
    )
    out = pl.pallas_call(
        unpack_kernel,
        out_shape=jax.ShapeDtypeStruct((1, doc_rows), F32),
        in_specs=in_vmem(2),
        out_specs=in_vmem(1)[0],
        compiler_params=pltpu.CompilerParams(vmem_limit_bytes=4 * MIB),
        name="unpack",
    )(docs, back)
    return out.reshape(doc_rows)


def solution(mesh):
    in_specs = (P(("dp", "pair"), None), P(), P())
    out_specs = P(("dp", "pair"))
    return jax.shard_map(body, mesh=mesh, in_specs=in_specs, out_specs=out_specs, check_vma=False)
```

```python
from functools import partial

import jax
import jax.numpy as jnp
from jax import lax
from jax.experimental import pallas as pl
from jax.experimental.pallas import tpu as pltpu
from jax.sharding import PartitionSpec as P

BF16 = jnp.bfloat16
F32 = jnp.float32
I32 = jnp.int32
MIB = 1024 * 1024
BOTH = ("dp", "pair")
FIRST = 37
LOW = 32


def iota(shape, dim):
    return lax.broadcasted_iota(I32, shape, dim)


def in_vmem(count):
    return [pl.BlockSpec(memory_space=pltpu.VMEM)] * count


def my_place():
    return lax.axis_index("dp").astype(I32), lax.axis_index("pair").astype(I32)


def chip_parity(chip):
    return ((chip >> 4) + (chip >> 2) + chip) & 1


def chip_position(chip):
    return chip >> 1


def listed(place):
    return (place + FIRST) & 63


def owner_chip(position):
    return 2 * position + (((position >> 3) + (position >> 1)) & 1)


def merge_twos(a, b):
    low, high = jnp.minimum(a[0], b[0]), jnp.maximum(a[1], b[1])
    return [
        jnp.maximum(a[0], b[0]), jnp.maximum(low, high), jnp.minimum(low, high), jnp.minimum(a[1], b[1])
    ]


def top_four(a, b):
    c = [jnp.maximum(x, y) for x, y in zip(a, b[::-1])]
    e, f = jnp.maximum(c[0], c[2]), jnp.maximum(c[1], c[3])
    g, h = jnp.minimum(c[0], c[2]), jnp.minimum(c[1], c[3])
    return [jnp.maximum(e, f), jnp.minimum(e, f), jnp.maximum(g, h), jnp.minimum(g, h)]


def pack_kernel(
    emb_hbm, ids_hbm, counts_hbm, packed_ref, doc_ref, emb_ref, ids_ref, counts_ref, sems
):
    copies = [
        pltpu.make_async_copy(counts_hbm, counts_ref, sems.at[0]),
        pltpu.make_async_copy(ids_hbm, ids_ref, sems.at[1]),
        pltpu.make_async_copy(emb_hbm, emb_ref, sems.at[2]),
    ]
    for copy in copies:
        copy.start()
    doc_rows = emb_ref.shape[0]
    clusters = ids_ref.shape[0] // 8
    doc_total = doc_rows * 2 * clusters
    chip, core = my_place()
    first = (chip * 2 + core) * doc_rows
    near_pair = chip_position(chip) ^ jnp.where(core == 0, 2, 0)
    turned = (chip_parity(chip) == 1) & (((near_pair - FIRST) & 63) >= LOW)
    flip = jnp.where(turned, jnp.where(core == 0, 10, 1), 0)
    diagonal = iota((clusters, clusters), 0) == iota((clusters, clusters), 1)
    even = iota((clusters, 1), 0) % 2 == 0
    lift = jnp.where(even, doc_rows, 0)
    even_wide = iota((clusters, 128), 0) % 2 == 0
    copies[0].wait()
    counts = jnp.sum(
        jnp.where(diagonal, jnp.broadcast_to(counts_ref[...], (clusters, clusters)), 0),
        axis=1,
        keepdims=True,
    )
    copies[1].wait()
    tiles = []
    for tile in range(8):
        ids = ids_ref[pl.ds(tile, clusters, stride=8), :]
        local = ids - first
        mine = (local >= 0) & (local < doc_rows) & (tile % 2 < counts) & (ids < doc_total)
        tiles.append(jnp.where(mine, local + lift, -1).astype(F32))
    twos = [(jnp.maximum(a, b), jnp.minimum(a, b)) for a, b in zip(tiles[::2], tiles[1::2])]
    fours = [merge_twos(a, b) for a, b in zip(twos[::2], twos[1::2])]
    mine_top = top_four(*fours)
    partner_top = [
        jnp.where(even_wide, pltpu.roll(a, clusters - 1, 0), pltpu.roll(a, 1, 0)) for a in mine_top
    ]
    ranked = top_four(mine_top, partner_top)
    ranked = [jnp.transpose(a) for a in ranked]
    doc_column = iota((doc_rows, clusters), 0).astype(F32)
    which = iota((clusters, clusters), 0)
    picked = jnp.zeros((clusters, clusters), F32)
    hits = []
    for rank in range(4):
        top = jnp.max(ranked[0], axis=0, keepdims=True)
        hit = ranked[0] == top
        ranked = [jnp.where(hit, b, a) for a, b in zip(ranked, ranked[1:])]
        doc = jnp.where(top >= doc_rows, top - doc_rows, top)
        picked = jnp.where(which == rank, doc, picked)
        hits.append((doc == doc_column).astype(BF16))
    pairs = clusters // 2
    rows = 4 * pairs
    row, spot = iota((rows, 4 * clusters), 0), iota((rows, 4 * clusters), 1)
    spread = (spot == (row & 3) * clusters + 2 * (listed(row >> 2) ^ flip)).astype(BF16)
    last = (((1,), (1,)), ((), ()))
    copies[2].wait()
    pick = lax.dot_general(
        spread, jnp.concatenate(hits, axis=1), last, preferred_element_type=F32
    ).astype(BF16)
    emb = emb_ref[...]
    square = jnp.sum(emb * emb, axis=1, keepdims=True)
    normed = (emb * lax.rsqrt(square + 1e-06)).astype(BF16)
    packed = jnp.dot(pick, normed, preferred_element_type=F32).astype(BF16)
    packed_ref[...] = packed.reshape(packed_ref.shape)
    take_pair = iota((pairs, clusters), 1) == 2 * listed(iota((pairs, clusters), 0))
    doc_ref[...] = lax.dot_general(
        take_pair.astype(BF16), picked.astype(BF16), last, preferred_element_type=F32
    ).astype(I32)


def in_hbm(array):
    return pltpu.with_memory_space_constraint(array, pltpu.HBM)


def pack(embeddings, block_ids, counts):
    clusters, blocks, block_rows = block_ids.shape
    tiles = block_rows // 128
    block_ids = block_ids.reshape(clusters, blocks, tiles, 128).transpose(0, 2, 1, 3)
    block_ids = block_ids.reshape(clusters * tiles * blocks, 128)
    embeddings, block_ids, counts = in_hbm(embeddings), in_hbm(block_ids), in_hbm(counts)
    doc_rows, feature = embeddings.shape
    return pl.pallas_call(
        pack_kernel,
        out_shape=(
            jax.ShapeDtypeStruct((clusters // 2, 4, feature), BF16),
            jax.ShapeDtypeStruct((clusters // 2, 128), I32),
        ),
        in_specs=[pl.BlockSpec(memory_space=pltpu.HBM)] * 3,
        out_specs=tuple(in_vmem(2)),
        scratch_shapes=[
            pltpu.VMEM(embeddings.shape, F32),
            pltpu.VMEM(block_ids.shape, I32),
            pltpu.VMEM(counts.shape, I32),
            pltpu.SemaphoreType.DMA((3,)),
        ],
        compiler_params=pltpu.CompilerParams(vmem_limit_bytes=24 * MIB),
        name="pack",
    )(embeddings, block_ids, counts)


def label_kernel(ids_hbm, counts_hbm, row_ref, col_ref, ids_ref, counts_ref, sems):
    blocks, block_rows = ids_ref.shape
    chip, core = my_place()
    cluster = 2 * chip_position(chip)
    ids_copy = pltpu.make_async_copy(ids_hbm.at[cluster], ids_ref, sems.at[0])
    counts_copy = pltpu.make_async_copy(counts_hbm, counts_ref, sems.at[1])
    ids_copy.start()
    counts_copy.start()
    group = iota((256, 1), 0)
    of_core = jnp.where(group < 128, core, 1 - core)
    hop = jnp.where(of_core == 0, 4, 1)
    base = owner_chip(listed(group & 63))
    source = jnp.where((group & 64) == 0, base, base ^ hop) * 2 + of_core
    counts_copy.wait()
    counts = counts_ref[...]
    count = jnp.sum(jnp.where(iota(counts.shape, 1) == cluster, counts, 0), axis=1, keepdims=True)
    ids_copy.wait()
    hits = jnp.zeros((256, block_rows), F32)
    for block in range(blocks):
        ids = ids_ref[block : block + 1, :]
        slot_source = jnp.where(block < count, ids >> 8, -1)
        hits = hits + jnp.where(source == slot_source, 1.0, 0.0)
    tally = jnp.sum(hits, axis=1, keepdims=True)
    tally_wide = jnp.broadcast_to(tally, (256, 128)).astype(BF16)
    col_spread = (iota((1024, 256), 0) // 4 == iota((1024, 256), 1)).astype(BF16)
    by_row = jnp.dot(col_spread, tally_wide, preferred_element_type=F32)
    rank = (iota((1024, 128), 0) % 4).astype(F32)
    col = jnp.where(rank >= by_row, 1.0, 0.0)
    col_ref[...] = col
    row_ref[...] = jnp.transpose(col[:512])[:8]


def labels(block_ids, counts):
    block_ids, counts = in_hbm(block_ids), in_hbm(counts)
    return pl.pallas_call(
        label_kernel,
        out_shape=(
            jax.ShapeDtypeStruct((8, 512), F32),
            jax.ShapeDtypeStruct((1024, 128), F32),
        ),
        in_specs=[pl.BlockSpec(memory_space=pltpu.HBM)] * 2,
        out_specs=tuple(in_vmem(2)),
        scratch_shapes=[
            pltpu.VMEM(block_ids.shape[1:], I32),
            pltpu.VMEM(counts.shape, I32),
            pltpu.SemaphoreType.DMA((2,)),
        ],
        compiler_params=pltpu.CompilerParams(vmem_limit_bytes=16 * MIB),
        cost_estimate=pl.CostEstimate(flops=10**9, bytes_accessed=4 * MIB, transcendentals=0),
        name="labels",
    )(block_ids, counts)


def column_best(others, own, other_label, own_label, offset=None):
    scores = lax.dot_general(others, own, (((1,), (1,)), ((), ())), preferred_element_type=F32)
    same = other_label == own_label
    if offset is not None:
        same = same & (iota(scores.shape, 0) + offset != iota(scores.shape, 1))
    return jnp.max(jnp.where(same, scores, -1.0), axis=0, keepdims=True)


def rows_of(*refs):
    rows = [ref[...].reshape(4 * ref.shape[0], ref.shape[2]) for ref in refs]
    return rows[0] if len(rows) == 1 else jnp.concatenate(rows, axis=0)


def direct_kernel(row_ref, col_ref, direct_ref, best_ref):
    own = rows_of(direct_ref)
    best = column_best(own, own, col_ref[0:256, 0:1], row_ref[0:1, 0:256], 0)
    best_ref[...] = jnp.broadcast_to(best, best_ref.shape)


def low_kernel(row_ref, col_ref, direct_ref, direct_other_ref, low_ref, before_ref, best_ref):
    end = 256 + 4 * LOW
    direct, low = rows_of(direct_ref), rows_of(low_ref)
    own = jnp.concatenate([direct, low], axis=0)
    label = row_ref[0:1, 0:end]
    best = jnp.maximum(
        column_best(low, own, col_ref[256:end, 0:1], label, 256),
        column_best(rows_of(direct_other_ref), own, col_ref[512:768, 0:1], label),
    )
    best_low = column_best(direct, low, col_ref[0:256, 0:1], row_ref[0:1, 256:end])
    best = jnp.maximum(best, jnp.concatenate([before_ref[0:1, :], best_low], axis=1))
    best_ref[...] = jnp.broadcast_to(best, best_ref.shape)


def high_kernel(
    row_ref,
    col_ref,
    direct_ref,
    direct_other_ref,
    low_ref,
    low_other_ref,
    high_ref,
    before_ref,
    best_ref,
    own_ref,
):
    start = 256 + 4 * LOW
    earlier, high = rows_of(direct_ref, low_ref), rows_of(high_ref)
    own = jnp.concatenate([earlier, high], axis=0)
    own_ref[...] = jnp.transpose(own)
    best = jnp.maximum(
        column_best(high, own, col_ref[start:512, 0:1], row_ref[0:1, :], start),
        column_best(rows_of(low_other_ref), own, col_ref[768 : start + 512, 0:1], row_ref[0:1, :]),
    )
    label = row_ref[0:1, start:512]
    best_high = jnp.maximum(
        column_best(earlier, high, col_ref[0:start, 0:1], label),
        column_best(rows_of(direct_other_ref), high, col_ref[512:768, 0:1], label),
    )
    best = jnp.maximum(best, jnp.concatenate([before_ref[0:1, :], best_high], axis=1))
    best_ref[...] = jnp.broadcast_to(best, best_ref.shape)


def final_kernel(row_ref, col_ref, own_ref, high_other_ref, before_ref, back_ref):
    start = 256 + 4 * LOW
    scores = jnp.dot(rows_of(high_other_ref), own_ref[...], preferred_element_type=F32)
    same = col_ref[start + 512 : 1024, 0:1] == row_ref[0:1, :]
    best = jnp.max(jnp.where(same, scores, -1.0), axis=0, keepdims=True)
    best = jnp.maximum(best, before_ref[0:1, :])
    slot, member = iota((128, 512), 0), iota((128, 512), 1)
    spread = jnp.where(member // 4 == slot, jnp.broadcast_to(best, (128, 512)), -1.0)
    for rank in range(4):
        back_ref[:, rank : rank + 1] = jnp.max(
            jnp.where(member % 4 == rank, spread, -1.0), axis=1, keepdims=True
        )


def vmem_call(kernel, shape, name, flops, *operands, wide=None):
    shapes = jax.ShapeDtypeStruct(shape, F32)
    places = in_vmem(1)[0]
    if wide is not None:
        shapes, places = (shapes, jax.ShapeDtypeStruct(wide, BF16)), tuple(in_vmem(2))
    return pl.pallas_call(
        kernel,
        out_shape=shapes,
        in_specs=in_vmem(len(operands)),
        out_specs=places,
        compiler_params=pltpu.CompilerParams(vmem_limit_bytes=16 * MIB),
        cost_estimate=pl.CostEstimate(flops=flops, bytes_accessed=2 * MIB, transcendentals=0),
        name=name,
    )(*operands)


def unpack_kernel(doc_ref, back_ref, out_ref):
    pairs = doc_ref.shape[0]
    doc_rows = out_ref.shape[1]
    doc_lane = iota((pairs, doc_rows), 1)
    top = jnp.full((pairs, doc_rows), -1.0, F32)
    for rank in range(4):
        hit = doc_ref[:, rank : rank + 1] == doc_lane
        top = jnp.maximum(top, jnp.where(hit, back_ref[0:pairs, rank : rank + 1], -1.0))
    out_ref[...] = jnp.max(top, axis=0, keepdims=True)


def chip_routes():
    owners = [owner_chip(listed(place)) for place in range(64)]
    direct, passing, back = [], [], []
    low, high, swap = [], [], []
    for core in range(2):
        near, far = (4, 16) if core == 0 else (1, 3)
        direct.append([chip * 2 + core for chip in owners])
        passing.append([(chip ^ near) * 2 + core for chip in owners])
        back.append(direct[-1] + passing[-1])
        for chip in range(128):
            low.append(((chip ^ near) * 2 + core, chip * 2 + core))
            high.append(((chip ^ far) * 2 + core, chip * 2 + core))
            swap.append((chip * 2 + core, chip * 2 + 1 - core))
    return direct + passing, back, low, high, swap


def body(embeddings, block_ids, block_counts):
    doc_rows = embeddings.shape[0]
    send_groups, back_groups, low_route, high_route, swap = chip_routes()
    counts = block_counts.reshape(1, -1)
    packed, docs = pack(embeddings, block_ids, counts)
    direct = lax.all_to_all(
        packed, BOTH, split_axis=0, concat_axis=0, axis_index_groups=send_groups, tiled=True
    )
    high = lax.ppermute(direct[LOW:], BOTH, high_route)
    low = lax.ppermute(direct[:LOW], BOTH, low_route)
    late_ids, late_counts, direct = lax.optimization_barrier((block_ids, counts, direct))
    row, col = labels(late_ids, late_counts)
    direct_other = lax.ppermute(direct, BOTH, swap)
    best = vmem_call(direct_kernel, (8, 256), "score_direct", 10**9, row, col, direct)
    low_other = lax.ppermute(low, BOTH, swap)
    best = vmem_call(
        low_kernel, (8, 256 + 4 * LOW), "score_low", 10**9,
        row, col, direct, direct_other, low, best,
    )
    high, best = lax.optimization_barrier((high, best))
    high_other = lax.ppermute(high, BOTH, swap)
    best, own = vmem_call(
        high_kernel, (8, 512), "score_high", 10**9,
        row, col, direct, direct_other, low, low_other, high, best,
        wide=(direct.shape[2], 512),
    )
    best = vmem_call(
        final_kernel, (128, 4), "score_final", 10**9,
        row, col, own, high_other, best,
    )
    back = lax.all_to_all(
        best, BOTH, split_axis=0, concat_axis=0, axis_index_groups=back_groups, tiled=True
    )
    out = pl.pallas_call(
        unpack_kernel,
        out_shape=jax.ShapeDtypeStruct((1, doc_rows), F32),
        in_specs=in_vmem(2),
        out_specs=in_vmem(1)[0],
        compiler_params=pltpu.CompilerParams(vmem_limit_bytes=4 * MIB),
        name="unpack",
    )(docs, back)
    return out.reshape(doc_rows)


def solution(mesh):
    in_specs = (P(("dp", "pair"), None), P(), P())
    out_specs = P(("dp", "pair"))
    return jax.shard_map(body, mesh=mesh, in_specs=in_specs, out_specs=out_specs, check_vma=False)
```
